128 devices in a mesh: lab: 8 (over z, core), leaf: 16 (over y, x).
Axes of the slice: x: 4, y: 4, z: 4, core: 2. Of those that a mesh axis runs over, the one named last changes fastest.
Arguments:
- query_tokens: int32 [4096, 32], P(('lab', 'leaf')), may hold values from 0 to 32767
- label_tokens: int32 [8192, 32], P(('lab', 'leaf')), may hold values from 0 to 32767
- label_node: int32 [8192], replicated, may hold values from 0 to 15, as said below
- shortlist_owner: int32 [4096, 8], P(('lab', 'leaf')), may hold values from 0 to 127, as said below
- shortlist_node: int32 [4096, 8, 8], P(('lab', 'leaf')), may hold values from 0 to 15, as said below
- positives: int32 [4096, 4], P(('lab', 'leaf')), may hold values from 0 to 8191, as said below
- token_lookup_table: bfloat16 [32768, 256], replicated, may hold values from -6 to 6
- width_three_filters: bfloat16 [768, 512], replicated, may hold values from -0.21875 to 0.21875
- width_five_filters: bfloat16 [1280, 512], replicated, may hold values from -0.15625 to 0.15625
- projection: bfloat16 [1024, 512], replicated, may hold values from -0.1875 to 0.1875
- free_vectors: bfloat16 [2048, 512], P(('lab', 'leaf')), may hold values from -4 to 4
Outputs:
- query_loss: float32 [4096], P(('lab', 'leaf'))
- grad_free: float32 [2048, 512], P(('lab', 'leaf'))
- grad_three: float32 [768, 512], P('leaf')
- grad_five: float32 [1280, 512], P('leaf')
- grad_projection: float32 [1024, 512], P('leaf')
The draws below stay inside these ranges and needn't reach their ends.
Inputs may be any that keep to these rules, and one draw needn't show every extreme that they name: `label_node`: every node of a device belongs to at least one of that device's 64 labels. `shortlist_owner`: the 8 owners of one query differ. Among the 32 queries of one device at most 8 name the same owner; one owner, the same on every device, is named by exactly 8 queries of every device. `shortlist_node`: the 8 nodes listed for one query and owner differ. `positives`: each positive label belongs to a node of its query's shortlist.
All inputs are finite; a program needn't handle non-finite values.
Results may differ from the reference program's by a relative error of at most 0.0035.
Values may be sent and summed in bfloat16 or wider, within the bound.
A program may use at most 128 MiB of HBM per device.

```python
import math
import jax
import jax.numpy as jnp
import numpy as np
from jax import lax

D = 512
EMB = 256
CH = 512
VOCAB = 32768
TLEN = 32
NODE_DEV = 16
K = 8
H = 8
P_SIZE = 4
Q_DEV = 32
L_DEV = 64
CAP = 8
QUERIES = 4096
LABELS = 8192
NODES = 2048
N_LAB = 8
N_LEAF = 16


def routing_plan(key):
    subkeys = jax.random.split(key, 9)
    devices = N_LAB * N_LEAF
    node_iota = jnp.arange(NODE_DEV, dtype=jnp.int32)
    raw_scores = jax.random.randint(subkeys[0], (devices, NODE_DEV), 0, 4096, dtype=jnp.int32)
    first_nodes = jnp.argsort(raw_scores * NODE_DEV + node_iota[None, :], axis=1).astype(jnp.int32)
    extra_nodes = jax.random.randint(subkeys[1], (devices, L_DEV - NODE_DEV), 0, NODE_DEV, dtype=jnp.int32)
    base_nodes = jnp.concatenate([first_nodes, extra_nodes], axis=1)
    label_iota = jnp.arange(L_DEV, dtype=jnp.int32)
    shuffle_scores = jax.random.randint(subkeys[2], (devices, L_DEV), 0, 4096, dtype=jnp.int32) * L_DEV + label_iota[None, :]
    shuffle = jnp.argsort(shuffle_scores, axis=1).astype(jnp.int32)
    label_node = jnp.take_along_axis(base_nodes, shuffle, axis=1)
    unshuffle = jnp.argsort(shuffle, axis=1).astype(jnp.int32)
    first_place = jnp.argsort(first_nodes, axis=1).astype(jnp.int32)
    hot_owner = jax.random.randint(subkeys[3], (), 0, devices, dtype=jnp.int32)
    owner_iota = jnp.arange(devices, dtype=jnp.int32)
    cold_scores = jax.random.randint(subkeys[4], (devices, devices), 0, 4096, dtype=jnp.int32) * devices + owner_iota[None, :]
    cold_scores = jnp.where(owner_iota[None, :] == hot_owner, 4096 * devices, cold_scores)
    cold_order = jnp.argsort(cold_scores, axis=1)[:, :devices - 1].astype(jnp.int32)
    query_iota = jnp.arange(Q_DEV, dtype=jnp.int32)[:, None]
    entry_iota = jnp.arange(K, dtype=jnp.int32)[None, :]
    hot_query = query_iota < CAP
    is_hot = hot_query & (entry_iota == 0)
    position = query_iota * K - jnp.minimum(query_iota, CAP) + entry_iota - hot_query.astype(jnp.int32)
    position = jnp.mod(position, devices - 1)
    cold_owner = cold_order[:, position.reshape(-1)].reshape(devices, Q_DEV, K)
    owners = jnp.where(is_hot[None, :, :], hot_owner, cold_owner)
    row_scores = jax.random.randint(subkeys[5], (devices, Q_DEV), 0, 4096, dtype=jnp.int32) * Q_DEV + jnp.arange(Q_DEV, dtype=jnp.int32)[None, :]
    row_shuffle = jnp.argsort(row_scores, axis=1).astype(jnp.int32)
    owners = jnp.take_along_axis(owners, row_shuffle[:, :, None], axis=1)
    entry_scores = jax.random.randint(subkeys[6], (devices, Q_DEV, K), 0, 4096, dtype=jnp.int32) * K + jnp.arange(K, dtype=jnp.int32)[None, None, :]
    entry_shuffle = jnp.argsort(entry_scores, axis=2).astype(jnp.int32)
    owners = jnp.take_along_axis(owners, entry_shuffle, axis=2).reshape(devices * Q_DEV, K)
    pick_scores = jax.random.randint(subkeys[7], (devices * Q_DEV, K, NODE_DEV), 0, 4096, dtype=jnp.int32) * NODE_DEV + node_iota[None, None, :]
    node_picks = jnp.argsort(pick_scores, axis=2)[:, :, :H].astype(jnp.int32)
    entry_pick = jax.random.randint(subkeys[8], (devices * Q_DEV, P_SIZE), 0, K, dtype=jnp.int32)
    slot_pick = jax.random.randint(jax.random.fold_in(subkeys[8], 1), (devices * Q_DEV, P_SIZE), 0, H, dtype=jnp.int32)
    positive_owner = jnp.take_along_axis(owners, entry_pick, axis=1)
    positive_node = jnp.take_along_axis(node_picks.reshape(devices * Q_DEV, K * H), entry_pick * H + slot_pick, axis=1)
    base_place = first_place[positive_owner, positive_node]
    label_place = unshuffle[positive_owner, base_place]
    positives = positive_owner * L_DEV + label_place
    return (label_node.reshape(-1), owners, node_picks, positives)


def draw_label_node(key, part):
    return routing_plan(key)[0]


def draw_shortlist_owner(key, part):
    return routing_plan(key)[1]


def draw_shortlist_node(key, part):
    return routing_plan(key)[2]


def draw_positives(key, part):
    return routing_plan(key)[3]


def plant(drawn, key, smallest, high):
    shape = drawn.shape
    index_at = [jax.random.randint(jax.random.fold_in(key, axis), (), 0, shape[axis]) for axis in range(len(shape))]
    drawn = drawn.at[tuple(index_at)].set(smallest)
    longest = shape.index(max(shape))
    index_at[longest] = (index_at[longest] + 1) % shape[longest]
    return drawn.at[tuple(index_at)].set(high)


def block_levels(stream_key, shape, pieces, least, largest):
    def one(dim, parts):
        draws = jax.random.uniform(jax.random.fold_in(jax.random.fold_in(stream_key, 6), dim), (parts,), jnp.float32, least / len(pieces), largest / len(pieces))
        return jnp.repeat(jnp.exp(draws), shape[dim] // parts).reshape((-1,) + (1,) * (len(shape) - dim - 1))

    gain = one(*pieces[0])
    for cut in pieces[1:]:
        gain = gain * one(*cut)
    return gain


def cumulative_ranks(number_of, slope):
    loads = [(1 << 20) // math.isqrt(grade ** slope) + 1 for grade in range(1, number_of + 1)]
    deviation = 1 + sum(loads) // (1 << 30)
    return np.cumsum(np.array([max(1, weight // deviation) for weight in loads]))


def ranked(own_key, extent, number_of, slope):
    table = cumulative_ranks(number_of, slope)
    ticket = jax.random.randint(jax.random.fold_in(own_key, 1), extent, 0, int(table[number_of - 1]))
    grade = jnp.searchsorted(jnp.asarray(table, jnp.int32), ticket, side="right")
    return jax.random.permutation(jax.random.fold_in(own_key, 2), number_of)[grade].astype(jnp.int32)


def gaussian(own_key, extent, scale, most, cuts=(), held_as=jnp.bfloat16):
    values = scale * jax.random.normal(own_key, extent, jnp.float32)
    if cuts:
        values = values * block_levels(own_key, extent, cuts, -0.22, 0.18)
    return jnp.clip(values, -most, most).astype(held_as)


def setup_inputs(seed: int = 0) -> dict:
    key_of = jax.random.split(jax.random.key(seed), 12)
    query_tokens = plant(ranked(key_of[0], (QUERIES, TLEN), VOCAB, 2), jax.random.fold_in(key_of[0], 3), 0, VOCAB - 1).astype(jnp.int32)
    label_tokens = plant(ranked(key_of[1], (LABELS, TLEN), VOCAB, 2), jax.random.fold_in(key_of[1], 3), 0, VOCAB - 1).astype(jnp.int32)
    label_node = draw_label_node(jax.random.fold_in(key_of[11], 71), 0)
    shortlist_owner = draw_shortlist_owner(jax.random.fold_in(key_of[11], 71), 0)
    shortlist_node = draw_shortlist_node(jax.random.fold_in(key_of[11], 71), 0)
    positives = draw_positives(jax.random.fold_in(key_of[11], 71), 0)
    token_lookup_table = gaussian(key_of[6], (VOCAB, EMB), 1.0, 6.0)
    width_three_filters = gaussian(key_of[7], (3 * EMB, CH), (3 * EMB) ** -0.5, 0.21875)
    width_five_filters = gaussian(key_of[8], (5 * EMB, CH), (5 * EMB) ** -0.5, 0.15625)
    projection = gaussian(key_of[9], (2 * CH, D), (2 * CH) ** -0.5, 0.1875)
    free_vectors = gaussian(key_of[10], (NODES, D), 0.3, 4.0, ((0, 128),))
    return {"query_tokens": query_tokens, "label_tokens": label_tokens, "label_node": label_node, "shortlist_owner": shortlist_owner, "shortlist_node": shortlist_node, "positives": positives, "token_lookup_table": token_lookup_table, "width_three_filters": width_three_filters, "width_five_filters": width_five_filters, "projection": projection, "free_vectors": free_vectors}


SCORE_SCALE = 0.25

def unfold(token_numbers, token_lookup_table, kernel_width):
    titles, length = token_numbers.shape
    embedded = jnp.take(token_lookup_table, token_numbers, axis=0)
    margin = kernel_width // 2
    padded = jnp.pad(embedded, ((0, 0), (margin, margin), (0, 0)))
    stacked = jnp.concatenate([padded[:, offset:offset + length, :] for offset in range(kernel_width)], axis=2)
    return stacked.reshape(titles * length, kernel_width * token_lookup_table.shape[1])

def gelu_tanh(values):
    return jax.nn.gelu(values, approximate=True)

def encode(token_numbers, token_lookup_table, width_three_filters, width_five_filters, projection):
    titles, length = token_numbers.shape
    three_taps = unfold(token_numbers, token_lookup_table, 3)
    five_taps = unfold(token_numbers, token_lookup_table, 5)
    preact = jnp.concatenate([jnp.dot(three_taps, width_three_filters, preferred_element_type=jnp.float32), jnp.dot(five_taps, width_five_filters, preferred_element_type=jnp.float32)], axis=1)
    pooled = lax.optimization_barrier(jnp.mean(gelu_tanh(preact).reshape(titles, length, -1), axis=1)).astype(jnp.bfloat16)
    encoded = jnp.dot(pooled, projection, preferred_element_type=jnp.float32)
    return (three_taps, five_taps, preact, pooled, encoded)

def backward_pass(token_numbers, grad_encoded, token_lookup_table, width_three_filters, width_five_filters, projection):
    three_taps, five_taps, preact, pooled, unused_enc = encode(token_numbers, token_lookup_table, width_three_filters, width_five_filters, projection)
    length = token_numbers.shape[1]
    channels = width_three_filters.shape[1]
    upstream = grad_encoded.astype(jnp.bfloat16)
    grad_projection = jnp.dot(pooled.T, upstream, preferred_element_type=jnp.float32)
    grad_pooled = jnp.dot(upstream, projection.T, preferred_element_type=jnp.float32)
    spread = jnp.repeat(grad_pooled / length, length, axis=0)
    unused_out, pullback = jax.vjp(gelu_tanh, preact)
    grad_preact = pullback(spread)[0].astype(jnp.bfloat16)
    grad_three = jnp.dot(three_taps.T, grad_preact[:, :channels], preferred_element_type=jnp.float32)
    grad_five = jnp.dot(five_taps.T, grad_preact[:, channels:], preferred_element_type=jnp.float32)
    return (grad_three, grad_five, grad_projection)

def reference(query_tokens, label_tokens, label_node, shortlist_owner, shortlist_node, positives, token_lookup_table, width_three_filters, width_five_filters, projection, free_vectors):

    def encode_block(token_numbers):
        return encode(token_numbers, token_lookup_table, width_three_filters, width_five_filters, projection)[4]
    query_encoded = lax.map(encode_block, query_tokens.reshape(-1, Q_DEV, TLEN)).reshape(QUERIES, D)
    label_encoded = lax.map(encode_block, label_tokens.reshape(-1, L_DEV, TLEN)).reshape(LABELS, D)
    query_rows = query_encoded.astype(jnp.bfloat16)
    label_ids = jnp.arange(LABELS, dtype=jnp.int32)
    label_home = label_ids // L_DEV * NODE_DEV + label_node
    node_sums = jax.ops.segment_sum(label_encoded, label_home, num_segments=NODES)
    node_counts = jax.ops.segment_sum(jnp.ones((LABELS,), jnp.float32), label_home, num_segments=NODES)
    head_rows = (node_sums / node_counts[:, None] + free_vectors.astype(jnp.float32)).astype(jnp.bfloat16)
    listed = (shortlist_owner[:, :, None] * NODE_DEV + shortlist_node).reshape(QUERIES, K * H)
    positive_home = positives // L_DEV * NODE_DEV + jnp.take(label_node, positives)
    targets = jnp.any(listed[:, :, None] == positive_home[:, None, :], axis=2).astype(jnp.float32)
    all_scores = SCORE_SCALE * jnp.dot(query_rows, head_rows.T, preferred_element_type=jnp.float32)
    scores = jnp.take_along_axis(all_scores, listed, axis=1)
    query_loss = lax.optimization_barrier(jnp.sum(jax.nn.softplus(scores) - targets * scores, axis=1))
    coefficient = SCORE_SCALE * (jax.nn.sigmoid(scores) - targets)
    query_index = jnp.arange(QUERIES, dtype=jnp.int32)[:, None]
    weighting = jnp.zeros((QUERIES, NODES), jnp.float32).at[query_index, listed].add(coefficient).astype(jnp.bfloat16)
    grad_free = jnp.dot(weighting.T, query_rows, preferred_element_type=jnp.float32)
    query_grad = jnp.dot(weighting, head_rows, preferred_element_type=jnp.float32)
    label_grad = grad_free[label_home] / node_counts[label_home][:, None]

    def accumulate(block_totals, batch_pair):
        token_numbers, gradient_block = batch_pair
        partial_terms = backward_pass(token_numbers, gradient_block, token_lookup_table, width_three_filters, width_five_filters, projection)
        return (tuple((running_total + partial_term for running_total, partial_term in zip(block_totals, partial_terms))), None)
    start_totals = (jnp.zeros((3 * EMB, CH), jnp.float32), jnp.zeros((5 * EMB, CH), jnp.float32), jnp.zeros((2 * CH, D), jnp.float32))
    block_totals, unused_q = lax.scan(accumulate, start_totals, (query_tokens.reshape(-1, Q_DEV, TLEN), query_grad.reshape(-1, Q_DEV, D)))
    block_totals, unused_l = lax.scan(accumulate, block_totals, (label_tokens.reshape(-1, L_DEV, TLEN), label_grad.reshape(-1, L_DEV, D)))
    return (query_loss, grad_free, block_totals[0], block_totals[1], block_totals[2])
```

```python
import jax
import jax.numpy as jnp
from jax import lax
from jax.sharding import PartitionSpec as P

SCORE_SCALE = 0.25


def gelu_tanh(values):
    return jax.nn.gelu(values, approximate=True)


def per_device(
    query_tokens,
    label_tokens,
    label_node,
    shortlist_owner,
    shortlist_node,
    positives,
    table,
    three,
    five,
    projection,
    free_vectors,
):
    axes = ("lab", "leaf")
    leaf_count = lax.axis_size("leaf")
    devices = lax.axis_size("lab") * leaf_count
    device_index = lax.axis_index("lab") * leaf_count + lax.axis_index("leaf")
    query_count, length = query_tokens.shape
    label_count = label_tokens.shape[0]
    node_count, width = free_vectors.shape
    emb = table.shape[1]
    channels = three.shape[1]
    nodes = devices * node_count
    titles = query_count + label_count

    listed = (shortlist_owner[:, :, None] * node_count + shortlist_node).reshape(query_count, -1)
    home = positives // label_count * node_count + jnp.take(label_node, positives)
    node_iota = jnp.arange(nodes, dtype=jnp.int32)
    is_listed = jnp.any(listed[:, :, None] == node_iota[None, None, :], axis=1)
    is_home = jnp.any(home[:, :, None] == node_iota[None, None, :], axis=1)
    code = is_listed.astype(jnp.bfloat16) * (1 + is_home.astype(jnp.bfloat16))
    code_out = code.reshape(query_count, devices, node_count).transpose(1, 2, 0)
    code_in = lax.all_to_all(code_out, axes, split_axis=0, concat_axis=0, tiled=True)
    owner_code = code_in.transpose(1, 0, 2).reshape(node_count, devices * query_count)

    tokens = jnp.concatenate([query_tokens, label_tokens], axis=0).T.reshape(-1)
    embedded = jnp.take(table, tokens, axis=0)
    margin = 2 * titles
    padded = jnp.pad(embedded, ((margin, margin), (0, 0)))
    rows = length * titles

    def taps(offset):
        return lax.slice_in_dim(padded, margin + offset * titles, margin + offset * titles + rows)

    five_taps = jnp.concatenate([taps(o) for o in (-2, -1, 0, 1, 2)], axis=1)
    three_taps = five_taps[:, emb : 4 * emb]
    pre3 = jnp.dot(three_taps, three, preferred_element_type=jnp.float32)
    pre5 = jnp.dot(five_taps, five, preferred_element_type=jnp.float32)

    def pool(v):
        return jnp.mean(gelu_tanh(v).reshape(length, titles, -1), axis=0).astype(jnp.bfloat16)

    pooled = jnp.concatenate([pool(pre3), pool(pre5)], axis=1)
    encoded = jnp.dot(pooled, projection, preferred_element_type=jnp.float32)
    query_rows = encoded[:query_count].astype(jnp.bfloat16)
    all_queries = lax.all_gather(query_rows, axes, axis=0, tiled=True)

    own_nodes = lax.dynamic_slice_in_dim(label_node, device_index * label_count, label_count)
    membership = (own_nodes[:, None] == jnp.arange(node_count, dtype=jnp.int32)[None, :]).astype(
        jnp.float32
    )
    counts = jnp.sum(membership, axis=0)
    sums = jnp.dot(
        membership.T,
        encoded[query_count:],
        precision=lax.Precision.HIGHEST,
        preferred_element_type=jnp.float32,
    )
    head_rows = (sums / counts[:, None] + free_vectors.astype(jnp.float32)).astype(jnp.bfloat16)
    all_heads = lax.all_gather(head_rows, axes, axis=0, tiled=True)

    def weigh(scores, code):
        target = (code > 1.5).astype(jnp.float32)
        live = (code > 0.5).astype(jnp.float32)
        coefficient = SCORE_SCALE * (jax.nn.sigmoid(scores) - target) * live
        return live, target, coefficient.astype(jnp.bfloat16)

    def dot_t(a, b):
        return lax.dot_general(a, b, (((1,), (1,)), ((), ())), preferred_element_type=jnp.float32)

    own_scores = SCORE_SCALE * dot_t(head_rows, all_queries)
    _, _, own_weights = weigh(own_scores, owner_code.astype(jnp.float32))
    grad_free = jnp.dot(own_weights, all_queries, preferred_element_type=jnp.float32)
    scores = SCORE_SCALE * dot_t(query_rows, all_heads)
    live, target, weights = weigh(scores, code.astype(jnp.float32))
    query_loss = jnp.sum(live * (jax.nn.softplus(scores) - target * scores), axis=1)
    query_grad = jnp.dot(weights, all_heads, preferred_element_type=jnp.float32)

    label_up = jnp.dot(
        membership.astype(jnp.bfloat16),
        (grad_free / counts[:, None]).astype(jnp.bfloat16),
        preferred_element_type=jnp.float32,
    ).astype(jnp.bfloat16)
    upstream = jnp.concatenate([query_grad.astype(jnp.bfloat16), label_up], axis=0)
    grad_projection = jnp.dot(pooled.T, upstream, preferred_element_type=jnp.float32)
    grad_pooled = dot_t(upstream, projection) / length

    def back(pre, part):
        pullback = jax.vjp(gelu_tanh, pre)[1]
        spread = jnp.broadcast_to(part[None], (length,) + part.shape).reshape(pre.shape)
        return pullback(spread)[0].astype(jnp.bfloat16)

    g3 = back(pre3, grad_pooled[:, :channels])
    g5 = back(pre5, grad_pooled[:, channels:])

    def finish(partial):
        part = lax.psum_scatter(partial, "leaf", scatter_dimension=0, tiled=True)
        return lax.psum(part, "lab")

    grad_three = jnp.dot(three_taps.T, g3, preferred_element_type=jnp.float32)
    grad_five = jnp.dot(five_taps.T, g5, preferred_element_type=jnp.float32)
    return (query_loss, grad_free, finish(grad_three), finish(grad_five), finish(grad_projection))


def solution(mesh):
    both = ("lab", "leaf")
    in_specs = (
        P(both, None),
        P(both, None),
        P(),
        P(both, None),
        P(both, None, None),
        P(both, None),
        P(),
        P(),
        P(),
        P(),
        P(both, None),
    )
    out_specs = (P(both), P(both, None), P("leaf", None), P("leaf", None), P("leaf", None))
    return jax.shard_map(
        per_device, mesh=mesh, in_specs=in_specs, out_specs=out_specs, check_vma=False
    )
```

```python
import jax
import jax.numpy as jnp
from jax import lax
from jax.experimental import pallas as pl
from jax.experimental.pallas import tpu as pltpu
from jax.sharding import PartitionSpec as P

MESH = pl.DeviceIdType.MESH
ORDERS = ("xyz", "yzx", "zxy")


SCORE_SCALE = 0.25


def where_am_i():
    lab, leaf = lax.axis_index("lab"), lax.axis_index("leaf")
    return {"z": lab // 2, "c": lab % 2, "y": leaf // 4, "x": leaf % 4}


def device_of(at):
    return (at["z"] * 2 + at["c"], at["y"] * 4 + at["x"])


def along(at, axis, step):
    size = 2 if axis == "c" else 4
    return {**at, axis: lax.rem(at[axis] + step, size)}


def greet(peers):
    barrier = pltpu.get_barrier_semaphore()
    for peer in peers:
        pl.semaphore_signal(barrier, inc=1, device_id=device_of(peer), device_id_type=MESH)
    pl.semaphore_wait(barrier, len(peers))


def gather_kernel(mine_ref, all_ref, local_sem, send_sem, recv_sem, pass_send, pass_recv):
    at = where_am_i()
    peers = [along(at, axis, d) for axis in "xyz" for d in (1, 2, 3)] + [along(at, "c", 1)]
    own = [
        pltpu.make_async_copy(
            mine_ref.at[part], all_ref.at[part, at["z"], at["c"], at["y"], at["x"]], local_sem.at[part]
        )
        for part in range(3)
    ]
    for copy in own:
        copy.start()
    greet(peers)
    for copy in own:
        copy.wait()

    def block(part, phase, place):
        done = ORDERS[part][:phase]
        index = [slice(None) if a in done else place[a] for a in "zyx"]
        return all_ref.at[part, index[0], place["c"], index[1], index[2]]

    def exchange(part, phase):
        axis = ORDERS[part][phase]
        copies = []
        for d in (1, 3, 2):
            slot = phase * 3 + d - 1
            here = block(part, phase, at)
            copies.append(
                pltpu.make_async_remote_copy(
                    src_ref=here,
                    dst_ref=here,
                    send_sem=send_sem.at[part, slot],
                    recv_sem=recv_sem.at[part, slot],
                    device_id=device_of(along(at, axis, d)),
                    device_id_type=MESH,
                )
            )
        return copies

    def hand_over(part, d):
        there = block(part, 2, along(at, ORDERS[part][2], 4 - d))
        return pltpu.make_async_remote_copy(
            src_ref=there,
            dst_ref=there,
            send_sem=pass_send.at[part, d],
            recv_sem=pass_recv.at[part, d],
            device_id=device_of(along(at, "c", 1)),
            device_id_type=MESH,
        )

    started = []
    stage = [exchange(part, 0) for part in range(3)]
    for copies in stage:
        for copy in copies:
            copy.start()
    for phase in (1, 2):
        later = []
        for part in range(3):
            for copy in stage[part]:
                copy.wait_recv()
            started += stage[part]
            copies = exchange(part, phase)
            for copy in copies:
                copy.start()
            if phase == 2:
                over = hand_over(part, 0)
                over.start()
                started_over.append(over)
            later.append(copies)
            if phase == 1:
                started_over = []
        stage = later
    for k, d in enumerate((1, 3, 2)):
        for part in range(3):
            stage[part][k].wait_recv()
            over = hand_over(part, d)
            over.start()
            started_over.append(over)
    for part in range(3):
        started += stage[part]
    for copy in started:
        copy.wait_send()
    for over in started_over:
        over.wait()


def gather_rows(mine):
    rows, width = mine.shape[1:]
    return pl.pallas_call(
        gather_kernel,
        out_shape=jax.ShapeDtypeStruct((3, 4, 2, 4, 4, rows, width), mine.dtype),
        in_specs=[pl.BlockSpec(memory_space=pltpu.VMEM)],
        out_specs=pl.BlockSpec(memory_space=pltpu.VMEM),
        scratch_shapes=[
            pltpu.SemaphoreType.DMA((3,)),
            pltpu.SemaphoreType.DMA((3, 9)),
            pltpu.SemaphoreType.DMA((3, 9)),
            pltpu.SemaphoreType.DMA((3, 4)),
            pltpu.SemaphoreType.DMA((3, 4)),
        ],
        compiler_params=pltpu.CompilerParams(
            collective_id=1, has_side_effects=True, vmem_limit_bytes=40 << 20
        ),
        name="gather_rows",
    )(mine)


def reduce_kernel(
    gp_ref, g5_ref, g3_ref, out_ref,
    half, other, r1, b, r2, c, r3, done,
    core_send, core_recv, send_sem, recv_sem, out_send, out_recv, local_sem,
):
    at = where_am_i()
    core = at["c"]
    partner = along(at, "c", 1)
    lab_steps = [(z, cc) for z in range(4) for cc in range(2)][1:]
    lab_peers = [along(along(at, "z", z), "c", cc) for z, cc in lab_steps]
    greet([along(at, axis, d) for axis in "xy" for d in (1, 2, 3)] + lab_peers)
    pieces = (
        (lambda k: gp_ref.at[:, :, k], 0, 0, 4),
        (lambda k: g5_ref.at[:, :, k, pl.ds(0, 4)], 1, 0, 4),
        (lambda k: g5_ref.at[:, :, k, pl.ds(4, 1)], 2, 0, 1),
        (lambda k: g3_ref.at[:, :, k], 2, 1, 3),
    )
    sent = []
    first = []
    for i, (view, part, row, rows) in enumerate(pieces):
        copy = pltpu.make_async_remote_copy(
            src_ref=view(1 - core),
            dst_ref=other.at[part, :, :, pl.ds(row, rows)],
            send_sem=core_send.at[i],
            recv_sem=core_recv.at[i],
            device_id=device_of(partner),
            device_id_type=MESH,
        )
        copy.start()
        first.append(copy)

    def send(part, phase, d, src, dst):
        slot = phase * 3 + d - 1
        copy = pltpu.make_async_remote_copy(
            src_ref=src,
            dst_ref=dst,
            send_sem=send_sem.at[part, slot],
            recv_sem=recv_sem.at[part, slot],
            device_id=device_of(along(at, ORDERS[part][phase], d)),
            device_id_type=MESH,
        )
        copy.start()
        sent.append(copy)
        return copy

    def pick(ref, part, axes, axis, place):
        index = [place if a == axis else slice(None) for a in axes]
        return ref.at[(part, *index)]

    def ship(part, phase, ref, axes, land):
        axis = ORDERS[part][phase]
        return [
            send(part, phase, d, pick(ref, part, axes, axis, lax.rem(at[axis] + d, 4)), land.at[part, d - 1])
            for d in (1, 3, 2)
        ]

    waiting = [None] * 3
    for i, (view, part, row, rows) in enumerate(pieces):
        first[i].wait_recv()
        mine = view(core)

        @pl.loop(0, 16)
        def _(leaf):
            yy, xx = leaf // 4, leaf % 4
            span = pl.ds(row, rows)
            half[part, yy, xx, span] = mine[yy, xx] + other[part, yy, xx, span]

        if i != 2:
            waiting[part] = ship(part, 0, half, "yxz", r1)
    sent += first

    for part in range(3):
        axis = ORDERS[part][0]
        left = "".join(a for a in "yxz" if a != axis)
        for copy in waiting[part]:
            copy.wait_recv()
        mine = pick(half, part, "yxz", axis, at[axis])

        @pl.loop(0, 4)
        def _(k):
            b[part, k] = (mine[k] + r1[part, 0, k]) + (r1[part, 1, k] + r1[part, 2, k])

        waiting[part] = ship(part, 1, b, left, r2)
    for part in range(3):
        axis = ORDERS[part][1]
        left = "".join(a for a in "yxz" if a not in ORDERS[part][:1])
        for copy in waiting[part]:
            copy.wait_recv()
        mine = pick(b, part, left, axis, at[axis])
        c[part] = (mine[...] + r2[part, 0]) + (r2[part, 1] + r2[part, 2])
        waiting[part] = ship(part, 2, c, ORDERS[part][2], r3)
    for part in range(3):
        axis = ORDERS[part][2]
        for copy in waiting[part]:
            copy.wait_recv()
        done[part] = (c[part, at[axis]] + r3[part, 0]) + (r3[part, 1] + r3[part, 2])
    own = pltpu.make_async_copy(done, out_ref.at[core, at["z"]], local_sem)
    own.start()
    final = []
    for i, peer in enumerate(lab_peers):
        copy = pltpu.make_async_remote_copy(
            src_ref=done,
            dst_ref=out_ref.at[core, at["z"]],
            send_sem=out_send.at[i],
            recv_sem=out_recv.at[i],
            device_id=device_of(peer),
            device_id_type=MESH,
        )
        copy.start()
        final.append(copy)
    own.wait()
    for copy in sent:
        copy.wait_send()
    for copy in final:
        copy.wait()


def reduce_gradients(gp, g5, g3):
    width = gp.shape[1]
    f32 = jnp.float32
    vmem = pl.BlockSpec(memory_space=pltpu.VMEM)
    out = pl.pallas_call(
        reduce_kernel,
        out_shape=jax.ShapeDtypeStruct((2, 4, 3, 8, width), f32),
        in_specs=[vmem] * 3,
        out_specs=vmem,
        scratch_shapes=[
            pltpu.VMEM((3, 4, 4, 4, 8, width), f32),
            pltpu.VMEM((3, 4, 4, 4, 8, width), f32),
            pltpu.VMEM((3, 3, 4, 4, 8, width), f32),
            pltpu.VMEM((3, 4, 4, 8, width), f32),
            pltpu.VMEM((3, 3, 4, 8, width), f32),
            pltpu.VMEM((3, 4, 8, width), f32),
            pltpu.VMEM((3, 3, 8, width), f32),
            pltpu.VMEM((3, 8, width), f32),
            pltpu.SemaphoreType.DMA((4,)),
            pltpu.SemaphoreType.DMA((4,)),
            pltpu.SemaphoreType.DMA((3, 9)),
            pltpu.SemaphoreType.DMA((3, 9)),
            pltpu.SemaphoreType.DMA((7,)),
            pltpu.SemaphoreType.DMA((7,)),
            pltpu.SemaphoreType.DMA,
        ],
        compiler_params=pltpu.CompilerParams(
            collective_id=2, has_side_effects=True, vmem_limit_bytes=40 << 20
        ),
        name="reduce_gradients",
    )(
        gp.reshape(4, 4, 2, 4, 8, width),
        g5.reshape(4, 4, 2, 5, 8, width),
        g3.reshape(4, 4, 2, 3, 8, width),
    )
    by_part = out.transpose(2, 0, 1, 3, 4)
    grad_projection = by_part[0].reshape(64, width)
    grad_five = jnp.concatenate([by_part[1], by_part[2][:, :1]], axis=1).reshape(80, width)
    grad_three = by_part[2][:, 1:].reshape(48, width)
    return grad_three, grad_five, grad_projection


def gelu_tanh(values):
    return jax.nn.gelu(values, approximate=True)


def per_device(
    query_tokens,
    label_tokens,
    label_node,
    shortlist_owner,
    shortlist_node,
    positives,
    table,
    three,
    five,
    projection,
    free_vectors,
):
    axes = ("lab", "leaf")
    leaf_count = lax.axis_size("leaf")
    devices = lax.axis_size("lab") * leaf_count
    device_index = lax.axis_index("lab") * leaf_count + lax.axis_index("leaf")
    query_count, length = query_tokens.shape
    label_count = label_tokens.shape[0]
    node_count, width = free_vectors.shape
    emb = table.shape[1]
    channels = three.shape[1]
    nodes = devices * node_count
    titles = query_count + label_count

    listed = (shortlist_owner[:, :, None] * node_count + shortlist_node).reshape(query_count, -1)
    home = positives // label_count * node_count + jnp.take(label_node, positives)
    node_iota = jnp.arange(nodes, dtype=jnp.int32)
    is_listed = jnp.any(listed[:, :, None] == node_iota[None, None, :], axis=1)
    is_home = jnp.any(home[:, :, None] == node_iota[None, None, :], axis=1)
    code = is_listed.astype(jnp.bfloat16) * (1 + is_home.astype(jnp.bfloat16))
    code_out = code.reshape(query_count, devices, node_count).transpose(1, 2, 0)
    code_in = lax.all_to_all(code_out, axes, split_axis=0, concat_axis=0, tiled=True)
    owner_code = code_in.reshape(devices, node_count, 2, 16).transpose(1, 2, 0, 3)
    owner_code = owner_code.reshape(node_count, devices * query_count)

    tokens = jnp.concatenate([query_tokens, label_tokens], axis=0).T.reshape(-1)
    embedded = jnp.take(table, tokens, axis=0)
    margin = 2 * titles
    padded = jnp.pad(embedded, ((margin, margin), (0, 0)))
    rows = length * titles

    def taps(offset):
        return lax.slice_in_dim(padded, margin + offset * titles, margin + offset * titles + rows)

    five_taps = jnp.concatenate([taps(o) for o in (-2, -1, 0, 1, 2)], axis=1)
    three_taps = five_taps[:, emb : 4 * emb]
    pre3 = jnp.dot(three_taps, three, preferred_element_type=jnp.float32)
    pre5 = jnp.dot(five_taps, five, preferred_element_type=jnp.float32)

    def pool(v):
        return jnp.mean(gelu_tanh(v).reshape(length, titles, -1), axis=0).astype(jnp.bfloat16)

    pooled = jnp.concatenate([pool(pre3), pool(pre5)], axis=1)
    encoded = jnp.dot(pooled, projection, preferred_element_type=jnp.float32)
    query_rows = encoded[:query_count].astype(jnp.bfloat16)

    own_nodes = lax.dynamic_slice_in_dim(label_node, device_index * label_count, label_count)
    membership = (own_nodes[:, None] == jnp.arange(node_count, dtype=jnp.int32)[None, :]).astype(
        jnp.float32
    )
    counts = jnp.sum(membership, axis=0)
    sums = jnp.dot(
        membership.T,
        encoded[query_count:],
        precision=lax.Precision.HIGHEST,
        preferred_element_type=jnp.float32,
    )
    head_rows = (sums / counts[:, None] + free_vectors.astype(jnp.float32)).astype(jnp.bfloat16)
    gathered = gather_rows(jnp.concatenate([query_rows, head_rows], axis=0).reshape(3, 16, width))
    all_queries = gathered[:2].reshape(2 * devices * 16, width)
    all_heads = gathered[2].reshape(nodes, width)

    def weigh(scores, code):
        target = (code > 1.5).astype(jnp.float32)
        live = (code > 0.5).astype(jnp.float32)
        coefficient = SCORE_SCALE * (jax.nn.sigmoid(scores) - target) * live
        return live, target, coefficient.astype(jnp.bfloat16)

    def dot_t(a, b):
        return lax.dot_general(a, b, (((1,), (1,)), ((), ())), preferred_element_type=jnp.float32)

    own_scores = SCORE_SCALE * dot_t(head_rows, all_queries)
    _, _, own_weights = weigh(own_scores, owner_code.astype(jnp.float32))
    grad_free = jnp.dot(own_weights, all_queries, preferred_element_type=jnp.float32)
    scores = SCORE_SCALE * dot_t(query_rows, all_heads)
    live, target, weights = weigh(scores, code.astype(jnp.float32))
    query_loss = jnp.sum(live * (jax.nn.softplus(scores) - target * scores), axis=1)
    query_grad = jnp.dot(weights, all_heads, preferred_element_type=jnp.float32)

    label_up = jnp.dot(
        membership.astype(jnp.bfloat16),
        (grad_free / counts[:, None]).astype(jnp.bfloat16),
        preferred_element_type=jnp.float32,
    ).astype(jnp.bfloat16)
    upstream = jnp.concatenate([query_grad.astype(jnp.bfloat16), label_up], axis=0)
    grad_projection = jnp.dot(pooled.T, upstream, preferred_element_type=jnp.float32)
    grad_pooled = dot_t(upstream, projection) / length

    def back(pre, part):
        pullback = jax.vjp(gelu_tanh, pre)[1]
        spread = jnp.broadcast_to(part[None], (length,) + part.shape).reshape(pre.shape)
        return pullback(spread)[0].astype(jnp.bfloat16)

    g3 = back(pre3, grad_pooled[:, :channels])
    g5 = back(pre5, grad_pooled[:, channels:])

    grad_three = jnp.dot(three_taps.T, g3, preferred_element_type=jnp.float32)
    grad_five = jnp.dot(five_taps.T, g5, preferred_element_type=jnp.float32)
    grad_three, grad_five, grad_projection = reduce_gradients(
        grad_projection, grad_five, grad_three
    )
    return (query_loss, grad_free, grad_three, grad_five, grad_projection)


def solution(mesh):
    both = ("lab", "leaf")
    in_specs = (
        P(both, None),
        P(both, None),
        P(),
        P(both, None),
        P(both, None, None),
        P(both, None),
        P(),
        P(),
        P(),
        P(),
        P(both, None),
    )
    out_specs = (P(both), P(both, None), P("leaf", None), P("leaf", None), P("leaf", None))
    return jax.shard_map(
        per_device, mesh=mesh, in_specs=in_specs, out_specs=out_specs, check_vma=False
    )
```

```python
import jax
import jax.numpy as jnp
from jax import lax
from jax.experimental import pallas as pl
from jax.experimental.pallas import tpu as pltpu
from jax.sharding import PartitionSpec as P

MESH = pl.DeviceIdType.MESH
ORDERS = ("xyz", "yzx", "zxy")


SCORE_SCALE = 0.25


def where_am_i():
    lab, leaf = lax.axis_index("lab"), lax.axis_index("leaf")
    return {"z": lab // 2, "c": lab % 2, "y": leaf // 4, "x": leaf % 4}


def device_of(at):
    return (at["z"] * 2 + at["c"], at["y"] * 4 + at["x"])


def along(at, axis, step):
    size = 2 if axis == "c" else 4
    return {**at, axis: lax.rem(at[axis] + step, size)}


ROOT = 0.7978845608028654
CUBIC = 0.044715
Q_PARTS = ((0, 256), (256, 256), (512, 128))
H_PARTS = ((0, 128), (128, 128), (256, 256))
STEPS = (1, 3, 2)


def window_kernel(
    emb_ref, w3_hbm, w5_hbm, proj_hbm, info_ref, row_ref, col_ref, free_vec_ref,
    loss_ref, free_ref, out_ref,
    w3_ref, w5_ref, proj_ref, taps, slope, total, pooled_ref,
    all_q, all_h, free_acc, grad_acc, loss_acc, tiles,
    grad_pre, gp_ref, g5_ref, g3_ref,
    half, other, r1, b, r2, c, r3, done,
    load_sem, q_send, q_recv, h_send, h_recv, over_send, over_recv,
    core_send, core_recv, send_sem, recv_sem, out_send, out_recv, local_sem,
):
    at = where_am_i()
    bf16, f32 = jnp.bfloat16, jnp.float32
    core = at["c"]
    partner = along(at, "c", 1)
    lab_steps = [(z, cc) for z in range(4) for cc in range(2)][1:]
    lab_peers = [along(along(at, "z", z), "c", cc) for z, cc in lab_steps]
    home = (at["z"], at["c"], at["y"], at["x"])
    queries = info_ref.shape[0]
    labels = col_ref.shape[0]
    nodes, width = free_vec_ref.shape
    rows, emb = emb_ref.shape
    length = rows // (queries + labels)
    q_rows = queries * length
    channels = w3_ref.shape[1]
    wide = all_q.shape[-1]

    loads = [
        pltpu.make_async_copy(src, dst, load_sem.at[i])
        for i, (src, dst) in enumerate(((w3_hbm, w3_ref), (w5_hbm, w5_ref), (proj_hbm, proj_ref)))
    ]
    for load in loads:
        load.start()

    def nt(a, b):
        return lax.dot_general(a, b, (((1,), (1,)), ((), ())), preferred_element_type=f32)

    def tn(a, b):
        return lax.dot_general(a, b, (((0,), (0,)), ((), ())), preferred_element_type=f32)

    def unfold(base, titles):
        size = titles * length
        for k in range(5):
            move = (k - 2) * titles
            low, high = max(0, -move), size - max(0, move)
            columns = pl.ds(k * emb, emb)
            if low:
                taps[pl.ds(base, low), columns] = jnp.zeros((low, emb), bf16)
            taps[pl.ds(base + low, high - low), columns] = emb_ref[pl.ds(base + low + move, high - low), :]
            if high < size:
                taps[pl.ds(base + high, size - high), columns] = jnp.zeros((size - high, emb), bf16)

    def convolve(base, titles, first):
        block = 512
        for col in range(0, 2 * channels, 256):
            if col < channels:
                pre = jnp.dot(
                    taps[pl.ds(base, block), emb : 4 * emb], w3_ref[:, col : col + 256],
                    preferred_element_type=f32,
                )
            else:
                pre = jnp.dot(
                    taps[pl.ds(base, block), :], w5_ref[:, col - channels : col - channels + 256],
                    preferred_element_type=f32,
                )
            bend = (ROOT * CUBIC) * (pre * pre)
            inner = bend + ROOT
            tanh = jnp.tanh(pre * inner)
            gate = 1.0 + tanh
            value = pre * gate
            slope[pl.ds(base, block), col : col + 256] = gate + value * (1.0 - tanh) * (inner + (bend + bend))
            part = jnp.sum(value.reshape(block // titles, titles, 256), axis=0)
            where = pl.ds(0 if titles == queries else queries, titles)
            if first:
                total[where, col : col + 256] = part
            else:
                total[where, col : col + 256] += part

    def encoded_of(where):
        pooled = (total[where, :] * (0.5 / length)).astype(bf16)
        pooled_ref[where, :] = pooled
        return jnp.dot(pooled, proj_ref[...], preferred_element_type=f32)

    def region(ref, part, phase, place, columns, spread=slice(None)):
        free = ORDERS[part][:phase]
        z, y, x = [slice(None) if a in free else place[a] for a in "zyx"]
        return ref.at[z, place["c"], y, x, spread, pl.ds(*columns)]

    started = []

    def push(ref, send, recv, slot, peer):
        copy = pltpu.make_async_remote_copy(
            src_ref=ref,
            dst_ref=ref,
            send_sem=send.at[slot],
            recv_sem=recv.at[slot],
            device_id=device_of(peer),
            device_id_type=MESH,
        )
        copy.start()
        started.append(copy)
        return copy

    def direct(ref, columns, send, recv, part, phase):
        here = region(ref, part, phase, at, columns[part])
        axis = ORDERS[part][phase]
        return [
            push(here, send, recv, (part, phase * 3 + d - 1), along(at, axis, d)) for d in STEPS
        ]

    def hand_over(ref, columns, group, part, d):
        there = region(ref, part, 2, along(at, ORDERS[part][2], d), columns[part])
        return push(there, over_send, over_recv, (group, part * 4 + d), partner)

    def wait_all(copies):
        for copy in copies:
            copy.wait_recv()

    barrier = pltpu.get_barrier_semaphore()
    peers = [along(at, axis, d) for axis in "xy" for d in (1, 2, 3)] + lab_peers
    for peer in peers:
        pl.semaphore_signal(barrier, inc=1, device_id=device_of(peer), device_id_type=MESH)
    unfold(0, queries)
    loads[0].wait()
    loads[1].wait()
    convolve(0, queries, True)
    convolve(512, queries, False)
    unfold(q_rows, labels)
    loads[2].wait()
    all_q[(*home, slice(None), pl.ds(0, width))] = encoded_of(pl.ds(0, queries)).astype(bf16)
    all_q[(*home, slice(None), pl.ds(width, wide - width))] = info_ref[...]
    pl.semaphore_wait(barrier, len(peers))
    q_stage = [direct(all_q, Q_PARTS, q_send, q_recv, part, 0) for part in range(3)]
    over = []

    convolve(q_rows, labels, True)
    for part in range(3):
        wait_all(q_stage[part])
        q_stage[part] = direct(all_q, Q_PARTS, q_send, q_recv, part, 1)
    convolve(q_rows + 512, labels, False)
    near = []
    for part in range(3):
        wait_all(q_stage[part])
        here = region(all_q, part, 2, at, Q_PARTS[part])
        axis = ORDERS[part][2]
        near.append(
            [push(here, q_send, q_recv, (part, 6 + k), along(at, axis, d)) for k, d in ((0, 1), (1, 3))]
        )
        over.append(hand_over(all_q, Q_PARTS, 0, part, 0))
    convolve(q_rows + 1024, labels, False)
    convolve(q_rows + 1536, labels, False)
    label_encoded = encoded_of(pl.ds(queries, labels))
    member = lax.broadcasted_iota(jnp.int32, (nodes, labels), 0) == row_ref[...]
    member = jnp.where(member, 1.0, 0.0)
    counts = jnp.sum(member, axis=1, keepdims=True)
    sums = jnp.dot(member, label_encoded, precision=lax.Precision.HIGHEST, preferred_element_type=f32)
    heads = (sums / counts + free_vec_ref[...].astype(f32)).astype(bf16)
    all_h[home] = heads
    h_stage = [direct(all_h, H_PARTS, h_send, h_recv, part, 0) for part in range(3)]
    far = []
    for part in range(3):
        axis = ORDERS[part][2]
        wait_all(near[part])
        for k, d in ((2, 1), (3, 3)):
            spread = pl.ds((k - 2) * (queries // 2), queries // 2)
            there = region(all_q, part, 2, along(at, axis, 4 - d), Q_PARTS[part], spread)
            far.append(push(there, q_send, q_recv, (part, 6 + k), along(at, axis, d)))
        over.append(hand_over(all_q, Q_PARTS, 0, part, 3))
        over.append(hand_over(all_q, Q_PARTS, 0, part, 1))
    for part in range(3):
        wait_all(h_stage[part])
        h_stage[part] = direct(all_h, H_PARTS, h_send, h_recv, part, 1)

    info = info_ref[...].astype(f32)
    lane = lax.rem(lax.broadcasted_iota(jnp.int32, (queries, 128), 1), nodes).astype(f32)
    for k in range(8):
        tile = jnp.zeros((queries, 128), f32)
        for h in range(8):
            code = info[:, k * 8 + h : k * 8 + h + 1]
            tile += jnp.where(code == lane, 1.0, 0.0) + jnp.where(code == lane + nodes, 2.0, 0.0)
        tiles[k] = tile

    for part in range(3):
        wait_all(far[2 * part : 2 * part + 2])
        over.append(hand_over(all_q, Q_PARTS, 0, part, 2))
    h_over = []
    for part in range(3):
        wait_all(h_stage[part])
        h_stage[part] = direct(all_h, H_PARTS, h_send, h_recv, part, 2)
        h_over.append(hand_over(all_h, H_PARTS, 1, part, 0))
    wait_all(over)

    me = ((at["z"] * 2 + at["c"]) * 16 + at["y"] * 4 + at["x"]).astype(f32)
    fold_row = lax.broadcasted_iota(jnp.int32, (8, 128), 0)
    fold_col = lax.broadcasted_iota(jnp.int32, (8, 128), 1)
    fold = jnp.where((lax.rem(fold_col, 8) == fold_row) & (fold_col < 64), 1.0, 0.0).astype(bf16)
    free_acc[...] = jnp.zeros_like(free_acc)
    grad_acc[...] = jnp.zeros_like(grad_acc)
    loss_acc[...] = jnp.zeros_like(loss_acc)
    node = lax.broadcasted_iota(jnp.int32, (nodes, 512), 0).astype(f32) + 1.0

    @pl.loop(0, 8)
    def _(i):
        chunk = all_q[i // 2, i % 2].reshape(512, wide)
        keys = chunk[:, :width]
        note = chunk[:, width:].astype(f32)
        owner = pltpu.roll(note, 64, 1)
        mine = jnp.where(owner == me, note + 1.0, 0.0).astype(bf16)
        listed = nt(fold, mine)
        scores = SCORE_SCALE * nt(all_h[home], keys)
        live = jnp.zeros((nodes, 512), f32)
        target = jnp.zeros((nodes, 512), f32)
        for h in range(8):
            entry = listed[h : h + 1]
            hit = jnp.where(entry == node + nodes, 1.0, 0.0)
            target += hit
            live += jnp.where(entry == node, 1.0, hit)
        weight = (SCORE_SCALE * (jax.nn.sigmoid(scores) - target) * live).astype(bf16)
        free_acc[...] += jnp.dot(weight, keys, preferred_element_type=f32)

    for k, d in enumerate(STEPS):
        for part in range(3):
            h_stage[part][k].wait_recv()
            h_over.append(hand_over(all_h, H_PARTS, 1, part, 4 - d))
    wait_all(h_over)

    own_rows = all_q[(*home, slice(None), pl.ds(0, width))]

    @pl.loop(0, 8)
    def _(i):
        keys = all_h[i // 2, i % 2].reshape(256, width)
        scores = SCORE_SCALE * nt(own_rows, keys)
        place = (lax.broadcasted_iota(jnp.int32, (queries, 256), 1) // nodes + i * (256 // nodes)).astype(f32)
        code = jnp.zeros((queries, 256), f32)
        for k in range(8):
            tile = tiles[k]
            pair = jnp.concatenate([tile, tile], axis=1)
            code += jnp.where(info[:, 64 + k * 8 : 65 + k * 8] == place, pair, 0.0)
        target = jnp.where(code > 1.5, 1.0, 0.0)
        live = jnp.where(code > 0.5, 1.0, 0.0)
        small = jnp.exp(-jnp.abs(scores))
        softplus = jnp.maximum(scores, 0.0) + jnp.log1p(small)
        loss_acc[...] += live * (softplus - target * scores)
        weight = (SCORE_SCALE * (jax.nn.sigmoid(scores) - target) * live).astype(bf16)
        grad_acc[...] += jnp.dot(weight, keys, preferred_element_type=f32)

    loss_ref[...] = jnp.broadcast_to(jnp.sum(loss_acc[...], axis=1, keepdims=True), loss_ref.shape)
    free = free_acc[...]
    free_ref[...] = free
    spread = jnp.where(lax.broadcasted_iota(jnp.int32, (labels, nodes), 1) == col_ref[...], 1.0, 0.0)
    label_up = jnp.dot(spread.astype(bf16), (free / counts).astype(bf16), preferred_element_type=f32)
    upstream = jnp.concatenate([grad_acc[...].astype(bf16), label_up.astype(bf16)], axis=0)

    sent = []
    first = {}
    pieces = (
        (lambda k: gp_ref.at[:, :, k], 0, 0, 4),
        (lambda k: g5_ref.at[:, :, k, pl.ds(0, 4)], 1, 0, 4),
        (lambda k: g5_ref.at[:, :, k, pl.ds(4, 1)], 2, 0, 1),
        (lambda k: g3_ref.at[:, :, k], 2, 1, 3),
    )

    def swap(i):
        view, part, row, count = pieces[i]
        copy = pltpu.make_async_remote_copy(
            src_ref=view(1 - core),
            dst_ref=other.at[part, :, :, pl.ds(row, count)],
            send_sem=core_send.at[i],
            recv_sem=core_recv.at[i],
            device_id=device_of(partner),
            device_id_type=MESH,
        )
        copy.start()
        first[i] = copy
        sent.append(copy)

    def join(i):
        view, part, row, count = pieces[i]
        first[i].wait_recv()
        mine = view(core)
        span = pl.ds(row, count)

        @pl.loop(0, 16)
        def _(leaf):
            yy, xx = leaf // 4, leaf % 4
            half[part, yy, xx, span] = mine[yy, xx] + other[part, yy, xx, span]

    def send(part, phase, d, src, dst):
        slot = phase * 3 + d - 1
        copy = pltpu.make_async_remote_copy(
            src_ref=src,
            dst_ref=dst,
            send_sem=send_sem.at[part, slot],
            recv_sem=recv_sem.at[part, slot],
            device_id=device_of(along(at, ORDERS[part][phase], d)),
            device_id_type=MESH,
        )
        copy.start()
        sent.append(copy)
        return copy

    def pick(ref, part, axes, axis, place):
        index = [place if a == axis else slice(None) for a in axes]
        return ref.at[(part, *index)]

    def ship(part, phase, ref, axes, land):
        axis = ORDERS[part][phase]
        return [
            send(part, phase, d, pick(ref, part, axes, axis, lax.rem(at[axis] + d, 4)), land.at[part, d - 1])
            for d in STEPS
        ]

    gp_ref[...] = tn(pooled_ref[...], upstream).reshape(gp_ref.shape)
    swap(0)
    grad_pooled = nt(upstream, proj_ref[...]) * (0.5 / length)

    def spread_back(low):
        for base, titles in ((0, queries), (q_rows, labels)):
            where = pl.ds(0 if titles == queries else queries, titles)
            mine = grad_pooled[:queries] if titles == queries else grad_pooled[queries:]
            mine = mine[:, low : low + channels]

            @pl.loop(0, length)
            def _(p):
                span = pl.ds(pl.multiple_of(base + p * titles, 32), titles)
                grad_pre[span, low : low + channels] = (
                    slope[span, low : low + channels] * mine
                ).astype(bf16)

    waiting = [None] * 3
    spread_back(channels)
    join(0)
    waiting[0] = ship(0, 0, half, "yxz", r1)
    for col in (0, 256):
        part = tn(taps[...], grad_pre[:, channels + col : channels + col + 256])
        g5_ref[:, :, :, :, :, col : col + 256] = part.reshape(g5_ref.shape[:-1] + (256,))
    swap(1)
    swap(2)
    spread_back(0)
    join(1)
    waiting[1] = ship(1, 0, half, "yxz", r1)
    for col in (0, 256):
        part = tn(taps[:, emb : 4 * emb], grad_pre[:, col : col + 256])
        g3_ref[:, :, :, :, :, col : col + 256] = part.reshape(g3_ref.shape[:-1] + (256,))
    swap(3)
    join(2)
    join(3)
    waiting[2] = ship(2, 0, half, "yxz", r1)

    for part in range(3):
        axis = ORDERS[part][0]
        left = "".join(a for a in "yxz" if a != axis)
        wait_all(waiting[part])
        mine = pick(half, part, "yxz", axis, at[axis])

        @pl.loop(0, 4)
        def _(k):
            b[part, k] = (mine[k] + r1[part, 0, k]) + (r1[part, 1, k] + r1[part, 2, k])

        waiting[part] = ship(part, 1, b, left, r2)
    for part in range(3):
        axis = ORDERS[part][1]
        left = "".join(a for a in "yxz" if a not in ORDERS[part][:1])
        wait_all(waiting[part])
        mine = pick(b, part, left, axis, at[axis])
        c[part] = (mine[...] + r2[part, 0]) + (r2[part, 1] + r2[part, 2])
        waiting[part] = ship(part, 2, c, ORDERS[part][2], r3)
    for part in range(3):
        axis = ORDERS[part][2]
        wait_all(waiting[part])
        done[part] = (c[part, at[axis]] + r3[part, 0]) + (r3[part, 1] + r3[part, 2])
    own = pltpu.make_async_copy(done, out_ref.at[core, at["z"]], local_sem)
    own.start()
    final = []
    for i, peer in enumerate(lab_peers):
        copy = pltpu.make_async_remote_copy(
            src_ref=done,
            dst_ref=out_ref.at[core, at["z"]],
            send_sem=out_send.at[i],
            recv_sem=out_recv.at[i],
            device_id=device_of(peer),
            device_id_type=MESH,
        )
        copy.start()
        final.append(copy)
    own.wait()
    for copy in started + sent:
        copy.wait_send()
    for copy in final:
        copy.wait()


def training_window(embedded, three, five, projection, info, own_row, own_col, free_vectors):
    rows, emb = embedded.shape
    channels = three.shape[1]
    nodes, width = free_vectors.shape
    queries, labels = info.shape[0], own_col.shape[0]
    titles = queries + labels
    f32, bf16 = jnp.float32, jnp.bfloat16
    vmem = pl.BlockSpec(memory_space=pltpu.VMEM)
    hbm = pl.BlockSpec(memory_space=pl.ANY)
    dma = pltpu.SemaphoreType.DMA
    loss, grad_free, out = pl.pallas_call(
        window_kernel,
        out_shape=(
            jax.ShapeDtypeStruct((queries, 128), f32),
            jax.ShapeDtypeStruct((nodes, width), f32),
            jax.ShapeDtypeStruct((2, 4, 3, 8, width), f32),
        ),
        in_specs=[vmem, hbm, hbm, hbm, vmem, vmem, vmem, vmem],
        out_specs=(vmem,) * 3,
        scratch_shapes=[
            pltpu.VMEM(three.shape, bf16),
            pltpu.VMEM(five.shape, bf16),
            pltpu.VMEM(projection.shape, bf16),
            pltpu.VMEM((rows, 5 * emb), bf16),
            pltpu.VMEM((rows, 2 * channels), f32),
            pltpu.VMEM((titles, 2 * channels), f32),
            pltpu.VMEM((titles, 2 * channels), bf16),
            pltpu.VMEM((4, 2, 4, 4, queries, width + 128), bf16),
            pltpu.VMEM((4, 2, 4, 4, nodes, width), bf16),
            pltpu.VMEM((nodes, width), f32),
            pltpu.VMEM((queries, width), f32),
            pltpu.VMEM((queries, 256), f32),
            pltpu.VMEM((8, queries, 128), f32),
            pltpu.VMEM((rows, 2 * channels), bf16),
            pltpu.VMEM((4, 4, 2, 4, 8, width), f32),
            pltpu.VMEM((4, 4, 2, 5, 8, width), f32),
            pltpu.VMEM((4, 4, 2, 3, 8, width), f32),
            pltpu.VMEM((3, 4, 4, 4, 8, width), f32),
            pltpu.VMEM((3, 4, 4, 4, 8, width), f32),
            pltpu.VMEM((3, 3, 4, 4, 8, width), f32),
            pltpu.VMEM((3, 4, 4, 8, width), f32),
            pltpu.VMEM((3, 3, 4, 8, width), f32),
            pltpu.VMEM((3, 4, 8, width), f32),
            pltpu.VMEM((3, 3, 8, width), f32),
            pltpu.VMEM((3, 8, width), f32),
            dma((3,)),
            dma((3, 10)),
            dma((3, 10)),
            dma((3, 9)),
            dma((3, 9)),
            dma((2, 12)),
            dma((2, 12)),
            dma((4,)),
            dma((4,)),
            dma((3, 9)),
            dma((3, 9)),
            dma((7,)),
            dma((7,)),
            dma,
        ],
        compiler_params=pltpu.CompilerParams(
            collective_id=1, has_side_effects=True, vmem_limit_bytes=60 << 20
        ),
        name="training_window",
    )(embedded, three, five, projection, info, own_row, own_col, free_vectors)
    by_part = out.transpose(2, 0, 1, 3, 4)
    grad_projection = by_part[0].reshape(64, width)
    grad_five = jnp.concatenate([by_part[1], by_part[2][:, :1]], axis=1).reshape(80, width)
    grad_three = by_part[2][:, 1:].reshape(48, width)
    return loss[:, 0], grad_free, grad_three, grad_five, grad_projection


def per_device(
    query_tokens,
    label_tokens,
    label_node,
    shortlist_owner,
    shortlist_node,
    positives,
    table,
    three,
    five,
    projection,
    free_vectors,
):
    device_index = lax.axis_index("lab") * lax.axis_size("leaf") + lax.axis_index("leaf")
    query_count = query_tokens.shape[0]
    label_count = label_tokens.shape[0]
    node_count = free_vectors.shape[0]

    positive_node = jnp.take(label_node, positives, mode="clip")
    home = positives // label_count * node_count + positive_node
    listed = shortlist_owner[:, :, None] * node_count + shortlist_node
    target = jnp.any(listed[:, :, :, None] == home[:, None, None, :], axis=3)
    codes = (shortlist_node + node_count * target.astype(jnp.int32)).reshape(query_count, -1)
    owners = jnp.broadcast_to(shortlist_owner[:, :, None], shortlist_node.shape).reshape(query_count, -1)
    info = jnp.concatenate([codes, owners], axis=1).astype(jnp.bfloat16)
    own_nodes = lax.dynamic_slice_in_dim(label_node, device_index * label_count, label_count)
    own_row, own_col = own_nodes[None, :], own_nodes[:, None]

    tokens = jnp.concatenate([query_tokens.T.reshape(-1), label_tokens.T.reshape(-1)])
    embedded = jnp.take(table, tokens, axis=0, mode="clip")
    return training_window(
        embedded, three, five, projection, info, own_row, own_col, free_vectors
    )


def solution(mesh):
    both = ("lab", "leaf")
    in_specs = (
        P(both, None),
        P(both, None),
        P(),
        P(both, None),
        P(both, None, None),
        P(both, None),
        P(),
        P(),
        P(),
        P(),
        P(both, None),
    )
    out_specs = (P(both), P(both, None), P("leaf", None), P("leaf", None), P("leaf", None))
    return jax.shard_map(
        per_device, mesh=mesh, in_specs=in_specs, out_specs=out_specs, check_vma=False
    )
```

```python
import jax
import jax.numpy as jnp
from jax import lax
from jax.experimental import pallas as pl
from jax.experimental.pallas import tpu as pltpu
from jax.sharding import PartitionSpec as P

MESH = pl.DeviceIdType.MESH
ORDERS = ("xyz", "yzx", "zxy")


SCORE_SCALE = 0.25


def where_am_i():
    lab, leaf = lax.axis_index("lab"), lax.axis_index("leaf")
    return {"z": lab // 2, "c": lab % 2, "y": leaf // 4, "x": leaf % 4}


def device_of(at):
    return (at["z"] * 2 + at["c"], at["y"] * 4 + at["x"])


def along(at, axis, step):
    size = 2 if axis == "c" else 4
    return {**at, axis: lax.rem(at[axis] + step, size)}


ROOT = 0.7978845608028654
CUBIC = 0.044715
Q_PARTS = ((0, 256), (256, 256), (512, 128))
H_PARTS = ((0, 128), (128, 128), (256, 256))
STEPS = (1, 3, 2)
WAVE_UNITS = (((0, 1), (1, 1), (2, 2)), ((0, 2), (2, 2), (4, 1)), ((0, 1), (1, 1), (2, 1)))


def shortlist_codes(nodes_ref, listed_ref, owner_ref, positive_ref, nodes, labels):
    bf16, f32 = jnp.bfloat16, jnp.float32
    count, queries = listed_ref.shape
    each = count // owner_ref.shape[0]
    listed = listed_ref[...]
    owners = jnp.concatenate(
        [jnp.broadcast_to(owner_ref[k : k + 1, :], (each, queries)) for k in range(count // each)], axis=0
    )
    table = nodes_ref[...].astype(f32).astype(bf16)
    lanes = table.shape[1]
    hit = jnp.zeros((count, queries), f32)
    for j in range(positive_ref.shape[0]):
        label = positive_ref[j : j + 1, :]
        row = lax.broadcasted_iota(jnp.int32, (table.shape[0], queries), 0) == label // lanes
        column = lax.broadcasted_iota(jnp.int32, (lanes, queries), 0) == label % lanes
        found = lax.dot_general(
            table, jnp.where(row, 1.0, 0.0).astype(bf16), (((0,), (0,)), ((), ())),
            preferred_element_type=f32,
        )
        node = jnp.sum(jnp.where(column, found, 0.0), axis=0, keepdims=True)
        same = (owners == label // labels) & (listed.astype(f32) == node)
        hit = jnp.where(same, 1.0, hit)
    codes = jnp.concatenate([listed.astype(f32) + nodes * hit, owners.astype(f32)], axis=0)
    square = (queries, queries)
    eye = lax.broadcasted_iota(jnp.int32, square, 0) == lax.broadcasted_iota(jnp.int32, square, 1)
    return lax.dot_general(
        jnp.where(eye, 1.0, 0.0).astype(bf16), codes.astype(bf16), (((1,), (1,)), ((), ())),
        preferred_element_type=f32,
    )


def window_kernel(
    emb_ref, w3_hbm, w5_hbm, proj_hbm, nodes_ref, listed_ref, owner_ref, positive_ref, free_vec_ref,
    loss_ref, free_ref, out3_ref, out5_ref, outp_ref,
    w3_ref, w5_ref, proj_ref, taps, slope, total, pooled_ref,
    all_q, all_h, free_acc, grad_acc, loss_acc, tiles,
    grad_pre, waves,
    load_sem, q_send, q_recv, h_send, h_recv, over_send, over_recv,
    core_send, core_recv, send_sem, recv_sem, out_send, out_recv,
):
    at = where_am_i()
    bf16, f32 = jnp.bfloat16, jnp.float32
    core = at["c"]
    partner = along(at, "c", 1)
    lab_steps = [(z, cc) for z in range(4) for cc in range(2)][1:]
    lab_peers = [along(along(at, "z", z), "c", cc) for z, cc in lab_steps]
    home = (at["z"], at["c"], at["y"], at["x"])
    queries, labels = listed_ref.shape[1], 64
    nodes, width = free_vec_ref.shape
    rows, emb = emb_ref.shape
    length = rows // (queries + labels)
    q_rows = queries * length
    channels = w3_ref.shape[1]
    wide = all_q.shape[-1]

    loads = [
        pltpu.make_async_copy(src, dst, load_sem.at[i])
        for i, (src, dst) in enumerate(((w3_hbm, w3_ref), (w5_hbm, w5_ref), (proj_hbm, proj_ref)))
    ]
    for load in loads:
        load.start()

    def nt(a, b):
        return lax.dot_general(a, b, (((1,), (1,)), ((), ())), preferred_element_type=f32)

    def tn(a, b):
        return lax.dot_general(a, b, (((0,), (0,)), ((), ())), preferred_element_type=f32)

    def unfold(base, titles):
        size = titles * length
        for k in range(5):
            move = (k - 2) * titles
            low, high = max(0, -move), size - max(0, move)
            columns = pl.ds(k * emb, emb)
            if low:
                taps[pl.ds(base, low), columns] = jnp.zeros((low, emb), bf16)
            taps[pl.ds(base + low, high - low), columns] = emb_ref[pl.ds(base + low + move, high - low), :]
            if high < size:
                taps[pl.ds(base + high, size - high), columns] = jnp.zeros((size - high, emb), bf16)

    def convolve(base, titles, first):
        block = 512
        for col in range(0, 2 * channels, 256):
            if col < channels:
                pre = jnp.dot(
                    taps[pl.ds(base, block), emb : 4 * emb], w3_ref[:, col : col + 256],
                    preferred_element_type=f32,
                )
            else:
                pre = jnp.dot(
                    taps[pl.ds(base, block), :], w5_ref[:, col - channels : col - channels + 256],
                    preferred_element_type=f32,
                )
            bend = (ROOT * CUBIC) * (pre * pre)
            inner = bend + ROOT
            tanh = jnp.tanh(pre * inner)
            gate = 1.0 + tanh
            value = pre * gate
            slope[pl.ds(base, block), col : col + 256] = gate + value * (1.0 - tanh) * (inner + (bend + bend))
            part = jnp.sum(value.reshape(block // titles, titles, 256), axis=0)
            where = pl.ds(0 if titles == queries else queries, titles)
            if first:
                total[where, col : col + 256] = part
            else:
                total[where, col : col + 256] += part

    def encoded_of(where):
        pooled = (total[where, :] * (0.5 / length)).astype(bf16)
        pooled_ref[where, :] = pooled
        return jnp.dot(pooled, proj_ref[...], preferred_element_type=f32)

    def region(ref, part, phase, place, columns, spread=slice(None)):
        free = ORDERS[part][:phase]
        z, y, x = [slice(None) if a in free else place[a] for a in "zyx"]
        return ref.at[z, place["c"], y, x, spread, pl.ds(*columns)]

    started = []

    def push(ref, send, recv, slot, peer):
        copy = pltpu.make_async_remote_copy(
            src_ref=ref,
            dst_ref=ref,
            send_sem=send.at[slot],
            recv_sem=recv.at[slot],
            device_id=device_of(peer),
            device_id_type=MESH,
        )
        copy.start()
        started.append(copy)
        return copy

    def direct(ref, columns, send, recv, part, phase):
        here = region(ref, part, phase, at, columns[part])
        axis = ORDERS[part][phase]
        return [
            push(here, send, recv, (part, phase * 3 + d - 1), along(at, axis, d)) for d in STEPS
        ]

    def hand_over(ref, columns, group, part, d):
        there = region(ref, part, 2, along(at, ORDERS[part][2], d), columns[part])
        return push(there, over_send, over_recv, (group, part * 4 + d), partner)

    def wait_all(copies):
        for copy in copies:
            copy.wait_recv()

    barrier = pltpu.get_barrier_semaphore()
    peers = [along(at, axis, d) for axis in "xy" for d in (1, 2, 3)] + lab_peers
    for peer in peers:
        pl.semaphore_signal(barrier, inc=1, device_id=device_of(peer), device_id_type=MESH)
    unfold(0, queries)
    loads[0].wait()
    loads[1].wait()
    convolve(0, queries, True)
    convolve(512, queries, False)
    unfold(q_rows, labels)
    loads[2].wait()
    info = shortlist_codes(nodes_ref, listed_ref, owner_ref, positive_ref, nodes, labels)
    all_q[(*home, slice(None), pl.ds(0, width))] = encoded_of(pl.ds(0, queries)).astype(bf16)
    all_q[(*home, slice(None), pl.ds(width, wide - width))] = info.astype(bf16)
    pl.semaphore_wait(barrier, len(peers))
    q_stage = [direct(all_q, Q_PARTS, q_send, q_recv, part, 0) for part in range(3)]
    over = []

    convolve(q_rows, labels, True)
    for part in range(3):
        wait_all(q_stage[part])
        q_stage[part] = direct(all_q, Q_PARTS, q_send, q_recv, part, 1)
    convolve(q_rows + 512, labels, False)
    near = []
    for part in range(3):
        wait_all(q_stage[part])
        here = region(all_q, part, 2, at, Q_PARTS[part])
        axis = ORDERS[part][2]
        near.append(
            [push(here, q_send, q_recv, (part, 6 + k), along(at, axis, d)) for k, d in ((0, 1), (1, 3))]
        )
        over.append(hand_over(all_q, Q_PARTS, 0, part, 0))
    convolve(q_rows + 1024, labels, False)
    convolve(q_rows + 1536, labels, False)
    label_encoded = encoded_of(pl.ds(queries, labels))
    index = at["z"] * 32 + at["c"] * 16 + at["y"] * 4 + at["x"]
    pair = jnp.broadcast_to(nodes_ref[pl.ds(index // 2, 1), :].astype(f32), (nodes, 2 * labels))
    pair = jnp.where(lax.rem(index, 2) == 0, pair, pltpu.roll(pair, labels, 1))[:, :labels]
    member = lax.broadcasted_iota(jnp.int32, (nodes, labels), 0).astype(f32) == pair
    member = jnp.where(member, 1.0, 0.0)
    counts = jnp.sum(member, axis=1, keepdims=True)
    sums = jnp.dot(member, label_encoded, precision=lax.Precision.HIGHEST, preferred_element_type=f32)
    heads = (sums / counts + free_vec_ref[...].astype(f32)).astype(bf16)
    all_h[home] = heads
    h_stage = [direct(all_h, H_PARTS, h_send, h_recv, part, 0) for part in range(3)]
    far = []
    for part in range(3):
        axis = ORDERS[part][2]
        wait_all(near[part])
        for k, d in ((2, 1), (3, 3)):
            spread = pl.ds((k - 2) * (queries // 2), queries // 2)
            there = region(all_q, part, 2, along(at, axis, 4 - d), Q_PARTS[part], spread)
            far.append(push(there, q_send, q_recv, (part, 6 + k), along(at, axis, d)))
        over.append(hand_over(all_q, Q_PARTS, 0, part, 3))
        over.append(hand_over(all_q, Q_PARTS, 0, part, 1))
    for part in range(3):
        wait_all(h_stage[part])
        h_stage[part] = direct(all_h, H_PARTS, h_send, h_recv, part, 1)

    lane = lax.rem(lax.broadcasted_iota(jnp.int32, (queries, 128), 1), nodes).astype(f32)
    for k in range(8):
        tile = jnp.zeros((queries, 128), f32)
        for h in range(8):
            code = info[:, k * 8 + h : k * 8 + h + 1]
            tile += jnp.where(code == lane, 1.0, 0.0) + jnp.where(code == lane + nodes, 2.0, 0.0)
        tiles[k] = tile

    for part in range(3):
        wait_all(far[2 * part : 2 * part + 2])
        over.append(hand_over(all_q, Q_PARTS, 0, part, 2))
    h_over = []
    for part in range(3):
        wait_all(h_stage[part])
        h_stage[part] = direct(all_h, H_PARTS, h_send, h_recv, part, 2)
        h_over.append(hand_over(all_h, H_PARTS, 1, part, 0))
    wait_all(over)

    me = index.astype(f32)
    fold_row = lax.broadcasted_iota(jnp.int32, (8, 128), 0)
    fold_col = lax.broadcasted_iota(jnp.int32, (8, 128), 1)
    fold = jnp.where((lax.rem(fold_col, 8) == fold_row) & (fold_col < 64), 1.0, 0.0).astype(bf16)
    free_acc[...] = jnp.zeros_like(free_acc)
    grad_acc[...] = jnp.zeros_like(grad_acc)
    loss_acc[...] = jnp.zeros_like(loss_acc)
    node = lax.broadcasted_iota(jnp.int32, (nodes, 512), 0).astype(f32) + 1.0

    @pl.loop(0, 8)
    def _(i):
        chunk = all_q[i // 2, i % 2].reshape(512, wide)
        keys = chunk[:, :width]
        note = chunk[:, width:].astype(f32)
        owner = pltpu.roll(note, 64, 1)
        mine = jnp.where(owner == me, note + 1.0, 0.0).astype(bf16)
        listed = nt(fold, mine)
        scores = SCORE_SCALE * nt(all_h[home], keys)
        live = jnp.zeros((nodes, 512), f32)
        target = jnp.zeros((nodes, 512), f32)
        for h in range(8):
            entry = listed[h : h + 1]
            hit = jnp.where(entry == node + nodes, 1.0, 0.0)
            target += hit
            live += jnp.where(entry == node, 1.0, hit)
        weight = (SCORE_SCALE * (jax.nn.sigmoid(scores) - target) * live).astype(bf16)
        free_acc[...] += jnp.dot(weight, keys, preferred_element_type=f32)

    for k, d in enumerate(STEPS):
        for part in range(3):
            h_stage[part][k].wait_recv()
            h_over.append(hand_over(all_h, H_PARTS, 1, part, 4 - d))
    wait_all(h_over)

    own_rows = all_q[(*home, slice(None), pl.ds(0, width))]

    @pl.loop(0, 8)
    def _(i):
        keys = all_h[i // 2, i % 2].reshape(256, width)
        scores = SCORE_SCALE * nt(own_rows, keys)
        place = (lax.broadcasted_iota(jnp.int32, (queries, 256), 1) // nodes + i * (256 // nodes)).astype(f32)
        code = jnp.zeros((queries, 256), f32)
        for k in range(8):
            tile = tiles[k]
            pair = jnp.concatenate([tile, tile], axis=1)
            code += jnp.where(info[:, 64 + k * 8 : 65 + k * 8] == place, pair, 0.0)
        target = jnp.where(code > 1.5, 1.0, 0.0)
        live = jnp.where(code > 0.5, 1.0, 0.0)
        small = jnp.exp(-jnp.abs(scores))
        softplus = jnp.maximum(scores, 0.0) + jnp.log1p(small)
        loss_acc[...] += live * (softplus - target * scores)
        weight = (SCORE_SCALE * (jax.nn.sigmoid(scores) - target) * live).astype(bf16)
        grad_acc[...] += jnp.dot(weight, keys, preferred_element_type=f32)

    loss = jnp.sum(loss_acc[...], axis=1, keepdims=True)
    same = (queries, queries)
    eye = lax.broadcasted_iota(jnp.int32, same, 0) == lax.broadcasted_iota(jnp.int32, same, 1)
    loss_ref[...] = jnp.sum(jnp.where(eye, loss, 0.0), axis=0, keepdims=True)
    free = free_acc[...]
    free_ref[...] = free
    label_up = tn(member.astype(bf16), (free / counts).astype(bf16))
    upstream = jnp.concatenate([grad_acc[...].astype(bf16), label_up.astype(bf16)], axis=0)

    sent = []
    lane_of = lambda place: pl.ds(pl.multiple_of(128 * place, 128), 128)

    def ship(wave, part, phase, view, land):
        axis = ORDERS[part][phase]
        copies = []
        for d in STEPS:
            slot = phase * 3 + d - 1
            copy = pltpu.make_async_remote_copy(
                src_ref=view(lax.rem(at[axis] + d, 4)),
                dst_ref=land.at[d - 1],
                send_sem=send_sem.at[wave * 3 + part, slot],
                recv_sem=recv_sem.at[wave * 3 + part, slot],
                device_id=device_of(along(at, axis, d)),
                device_id_type=MESH,
            )
            copy.start()
            copies.append(copy)
        sent.extend(copies)
        return copies

    def add(target, mine, land, steps):
        @pl.loop(0, steps)
        def _(k):
            target[k] = (mine(k) + land[0, k]) + (land[1, k] + land[2, k])

    def reduce_wave(wave, out_ref):
        own, other, done, parts = waves[wave]
        swap = pltpu.make_async_remote_copy(
            src_ref=own.at[:, :, 1 - core],
            dst_ref=other,
            send_sem=core_send.at[wave],
            recv_sem=core_recv.at[wave],
            device_id=device_of(partner),
            device_id_type=MESH,
        )
        swap.start()
        sent.append(swap)
        yield
        swap.wait_recv()

        @pl.loop(0, 16)
        def _(leaf):
            yy, xx = leaf // 4, leaf % 4
            own[yy, xx, core] += other[yy, xx]

        x, y, z = at["x"], at["y"], at["z"]
        us = [pl.ds(*units) for units in WAVE_UNITS[wave]]
        mine = own.at[:, :, core]
        (r1x, bx, r2x, cx, r3x), (r1y, by, r2y, cy, r3y), (r1z, bz, r2z, cz, r3z) = parts
        waiting = [
            ship(wave, 0, 0, lambda p: own.at[:, p, core, us[0]], r1x),
            ship(wave, 1, 0, lambda p: own.at[p, :, core, us[1]], r1y),
            ship(wave, 2, 0, lambda p: own.at[:, :, core, us[2], :, lane_of(p)], r1z),
        ]
        yield
        wait_all(waiting[0])
        add(bx, lambda k: own[k, x, core, us[0]], r1x, 4)
        waiting[0] = ship(wave, 0, 1, lambda p: bx.at[p], r2x)
        wait_all(waiting[1])
        add(by, lambda k: own[y, k, core, us[1]], r1y, 4)
        waiting[1] = ship(wave, 1, 1, lambda p: by.at[:, :, :, lane_of(p)], r2y)
        wait_all(waiting[2])
        for xx in range(4):

            @pl.loop(0, 4)
            def _(k, xx=xx):
                first = own[k, xx, core, us[2], :, lane_of(z)]
                bz[k, xx] = (first + r1z[0, k, xx]) + (r1z[1, k, xx] + r1z[2, k, xx])

        waiting[2] = ship(wave, 2, 1, lambda p: bz.at[:, p], r2z)
        yield
        wait_all(waiting[0])
        cx[...] = (bx[y] + r2x[0]) + (r2x[1] + r2x[2])
        waiting[0] = ship(wave, 0, 2, lambda p: cx.at[:, :, lane_of(p)], r3x)
        wait_all(waiting[1])
        add(cy, lambda k: by[k, :, :, lane_of(z)], r2y, 4)
        waiting[1] = ship(wave, 1, 2, lambda p: cy.at[p], r3y)
        wait_all(waiting[2])
        add(cz, lambda k: bz[k, x], r2z, 4)
        waiting[2] = ship(wave, 2, 2, lambda p: cz.at[p], r3z)
        yield
        wait_all(waiting[0])
        done[us[0]] = (cx[:, :, lane_of(z)] + r3x[0]) + (r3x[1] + r3x[2])
        wait_all(waiting[1])
        done[us[1]] = (cy[x] + r3y[0]) + (r3y[1] + r3y[2])
        wait_all(waiting[2])
        done[us[2]] = (cz[y] + r3z[0]) + (r3z[1] + r3z[2])
        place = out_ref.at[core, :, :, lane_of(z)]
        final = []
        for i, peer in enumerate(lab_peers):
            copy = pltpu.make_async_remote_copy(
                src_ref=done,
                dst_ref=place,
                send_sem=out_send.at[wave, i],
                recv_sem=out_recv.at[wave, i],
                device_id=device_of(peer),
                device_id_type=MESH,
            )
            copy.start()
            final.append(copy)
        out_ref[core, :, :, lane_of(z)] = done[...]
        yield
        for copy in final:
            copy.wait()
        yield

    gp_ref, g5_ref, g3_ref = (waves[i][0] for i in range(3))
    gp_ref[...] = tn(pooled_ref[...], upstream).reshape(gp_ref.shape)
    move_p = reduce_wave(0, outp_ref)
    next(move_p)
    grad_pooled = nt(upstream, proj_ref[...]) * (0.5 / length)

    def spread_back(low):
        for base, titles in ((0, queries), (q_rows, labels)):
            where = pl.ds(0 if titles == queries else queries, titles)
            mine = grad_pooled[:queries] if titles == queries else grad_pooled[queries:]
            mine = mine[:, low : low + channels]

            @pl.loop(0, length)
            def _(p):
                span = pl.ds(pl.multiple_of(base + p * titles, 32), titles)
                grad_pre[span, low : low + channels] = (
                    slope[span, low : low + channels] * mine
                ).astype(bf16)

    def weigh(ref, left, low):
        right = grad_pre[:, low : low + 256]
        col = low % channels
        ref[:, :, :, :, :, col : col + 256] = tn(left(), right).reshape(ref.shape[:-1] + (256,))

    spread_back(channels)
    next(move_p)
    weigh(g5_ref, lambda: taps[...], channels)
    weigh(g5_ref, lambda: taps[...], channels + 256)
    move_5 = reduce_wave(1, out5_ref)
    next(move_5)
    next(move_p)
    spread_back(0)
    next(move_5)
    weigh(g3_ref, lambda: taps[:, emb : 4 * emb], 0)
    next(move_p)
    weigh(g3_ref, lambda: taps[:, emb : 4 * emb], 256)
    move_3 = reduce_wave(2, out3_ref)
    next(move_3)
    next(move_p)
    next(move_5)
    next(move_3)
    next(move_5)
    next(move_3)
    next(move_5)
    next(move_3)
    next(move_3)
    for move in (move_p, move_5, move_3):
        next(move)
    for copy in started + sent:
        copy.wait_send()


def copy_out_kernel(*refs):
    for source, target in zip(refs[: len(refs) // 2], refs[len(refs) // 2 :]):
        target[...] = source[...]


def wave_scratch(units, width):
    f32 = jnp.float32
    count = sum(n for _, n in units)
    nx, ny, nz = (n for _, n in units)

    def pads(*shapes):
        return [pltpu.VMEM(shape, f32) for shape in shapes]

    return [
        pltpu.VMEM((4, 4, 2, count, 8, width), f32),
        pltpu.VMEM((4, 4, count, 8, width), f32),
        pltpu.VMEM((count, 8, 128), f32),
        [
            pads((3, 4, nx, 8, width), (4, nx, 8, width), (3, nx, 8, width), (nx, 8, width), (3, nx, 8, 128)),
            pads((3, 4, ny, 8, width), (4, ny, 8, width), (3, 4, ny, 8, 128), (4, ny, 8, 128), (3, ny, 8, 128)),
            pads(
                (3, 4, 4, nz, 8, 128), (4, 4, nz, 8, 128), (3, 4, nz, 8, 128), (4, nz, 8, 128), (3, nz, 8, 128)
            ),
        ],
    ]


def training_window(embedded, three, five, projection, label_node, listed, owner, positives, free_vectors):
    rows, emb = embedded.shape
    channels = three.shape[1]
    nodes, width = free_vectors.shape
    queries = listed.shape[1]
    titles = queries + 64
    f32, bf16 = jnp.float32, jnp.bfloat16
    vmem = pl.BlockSpec(memory_space=pltpu.VMEM)
    hbm = pl.BlockSpec(memory_space=pl.ANY)
    dma = pltpu.SemaphoreType.DMA
    shapes = (
        jax.ShapeDtypeStruct((1, queries), f32),
        jax.ShapeDtypeStruct((nodes, width), f32),
        jax.ShapeDtypeStruct((2, 3, 8, width), f32),
        jax.ShapeDtypeStruct((2, 5, 8, width), f32),
        jax.ShapeDtypeStruct((2, 4, 8, width), f32),
    )
    outs = pl.pallas_call(
        window_kernel,
        out_shape=shapes,
        in_specs=[vmem, hbm, hbm, hbm, vmem, vmem, vmem, vmem, vmem],
        out_specs=(vmem,) * 5,
        scratch_shapes=[
            pltpu.VMEM(three.shape, bf16),
            pltpu.VMEM(five.shape, bf16),
            pltpu.VMEM(projection.shape, bf16),
            pltpu.VMEM((rows, 5 * emb), bf16),
            pltpu.VMEM((rows, 2 * channels), f32),
            pltpu.VMEM((titles, 2 * channels), f32),
            pltpu.VMEM((titles, 2 * channels), bf16),
            pltpu.VMEM((4, 2, 4, 4, queries, width + 128), bf16),
            pltpu.VMEM((4, 2, 4, 4, nodes, width), bf16),
            pltpu.VMEM((nodes, width), f32),
            pltpu.VMEM((queries, width), f32),
            pltpu.VMEM((queries, 256), f32),
            pltpu.VMEM((8, queries, 128), f32),
            pltpu.VMEM((rows, 2 * channels), bf16),
            [wave_scratch(units, width) for units in WAVE_UNITS],
            dma((3,)),
            dma((3, 10)),
            dma((3, 10)),
            dma((3, 9)),
            dma((3, 9)),
            dma((2, 12)),
            dma((2, 12)),
            dma((3,)),
            dma((3,)),
            dma((9, 9)),
            dma((9, 9)),
            dma((3, 7)),
            dma((3, 7)),
        ],
        compiler_params=pltpu.CompilerParams(
            collective_id=1, has_side_effects=True, vmem_limit_bytes=60 << 20
        ),
        name="training_window",
    )(embedded, three, five, projection, label_node, listed, owner, positives, free_vectors)
    loss, grad_free, grad_three, grad_five, grad_projection = pl.pallas_call(
        copy_out_kernel,
        out_shape=shapes,
        in_specs=[vmem] * 5,
        out_specs=(vmem,) * 5,
        name="copy_out",
    )(*outs)
    return (
        loss.reshape(queries),
        grad_free,
        grad_three.reshape(48, width),
        grad_five.reshape(80, width),
        grad_projection.reshape(64, width),
    )


def per_device(
    query_tokens,
    label_tokens,
    label_node,
    shortlist_owner,
    shortlist_node,
    positives,
    table,
    three,
    five,
    projection,
    free_vectors,
):
    tokens = jnp.concatenate([query_tokens.T.reshape(-1), label_tokens.T.reshape(-1)])
    embedded = jnp.take(table, tokens, axis=0, mode="clip")
    return training_window(
        embedded,
        three,
        five,
        projection,
        label_node.reshape(-1, 128),
        shortlist_node.transpose(1, 2, 0).reshape(-1, query_tokens.shape[0]),
        shortlist_owner.T,
        positives.T,
        free_vectors,
    )


def solution(mesh):
    both = ("lab", "leaf")
    in_specs = (
        P(both, None),
        P(both, None),
        P(),
        P(both, None),
        P(both, None, None),
        P(both, None),
        P(),
        P(),
        P(),
        P(),
        P(both, None),
    )
    out_specs = (P(both), P(both, None), P("leaf", None), P("leaf", None), P("leaf", None))
    return jax.shard_map(
        per_device, mesh=mesh, in_specs=in_specs, out_specs=out_specs, check_vma=False
    )
```

```python
import jax
import jax.numpy as jnp
from jax import lax
from jax.experimental import pallas as pl
from jax.experimental.pallas import tpu as pltpu
from jax.sharding import PartitionSpec as P

MESH = pl.DeviceIdType.MESH
ORDERS = ("xyz", "yzx", "zxy")


SCORE_SCALE = 0.25


def where_am_i():
    lab, leaf = lax.axis_index("lab"), lax.axis_index("leaf")
    return {"z": lab // 2, "c": lab % 2, "y": leaf // 4, "x": leaf % 4}


def device_of(at):
    return (at["z"] * 2 + at["c"], at["y"] * 4 + at["x"])


def along(at, axis, step):
    size = 2 if axis == "c" else 4
    return {**at, axis: lax.rem(at[axis] + step, size)}


ROOT = 0.7978845608028654
CUBIC = 0.044715
Q_PARTS = ((0, 256), (256, 256), (512, 128))
H_PARTS = ((0, 128), (128, 128), (256, 256))
STEPS = (1, 3, 2)
WAVE_UNITS = (((0, 1), (1, 1), (2, 2)), ((0, 2), (2, 2), (4, 1)), ((0, 1), (1, 1), (2, 1)))


def shortlist_codes(nodes_ref, listed_ref, owner_ref, positive_ref, nodes, labels):
    bf16, f32 = jnp.bfloat16, jnp.float32
    count, queries = listed_ref.shape
    each = count // owner_ref.shape[0]
    listed = listed_ref[...]
    owners = jnp.concatenate(
        [jnp.broadcast_to(owner_ref[k : k + 1, :], (each, queries)) for k in range(count // each)], axis=0
    )
    table = nodes_ref[...].astype(f32).astype(bf16)
    lanes = table.shape[1]
    hit = jnp.zeros((count, queries), f32)
    for j in range(positive_ref.shape[0]):
        label = positive_ref[j : j + 1, :]
        row = lax.broadcasted_iota(jnp.int32, (table.shape[0], queries), 0) == label // lanes
        column = lax.broadcasted_iota(jnp.int32, (lanes, queries), 0) == label % lanes
        found = lax.dot_general(
            table, jnp.where(row, 1.0, 0.0).astype(bf16), (((0,), (0,)), ((), ())),
            preferred_element_type=f32,
        )
        node = jnp.sum(jnp.where(column, found, 0.0), axis=0, keepdims=True)
        same = (owners == label // labels) & (listed.astype(f32) == node)
        hit = jnp.where(same, 1.0, hit)
    codes = jnp.concatenate([listed.astype(f32) + nodes * hit, owners.astype(f32)], axis=0)
    square = (queries, queries)
    eye = lax.broadcasted_iota(jnp.int32, square, 0) == lax.broadcasted_iota(jnp.int32, square, 1)
    return lax.dot_general(
        jnp.where(eye, 1.0, 0.0).astype(bf16), codes.astype(bf16), (((1,), (1,)), ((), ())),
        preferred_element_type=f32,
    )


def window_kernel(
    emb_ref, w3_hbm, w5_hbm, proj_hbm, nodes_ref, listed_ref, owner_ref, positive_ref, free_vec_ref,
    loss_ref, free_ref, out3_ref, out5_ref, outp_ref,
    w3_ref, w5_ref, proj_ref, taps, slope, total, pooled_ref,
    all_q, all_h, free_acc, grad_acc, loss_acc, tiles,
    grad_pre, waves,
    load_sem, q_send, q_recv, h_send, h_recv, over_send, over_recv,
    core_send, core_recv, send_sem, recv_sem, out_send, out_recv,
):
    at = where_am_i()
    bf16, f32 = jnp.bfloat16, jnp.float32
    core = at["c"]
    partner = along(at, "c", 1)
    lab_steps = [(z, cc) for z in range(4) for cc in range(2)][1:]
    lab_peers = [along(along(at, "z", z), "c", cc) for z, cc in lab_steps]
    home = (at["z"], at["c"], at["y"], at["x"])
    queries, labels = listed_ref.shape[1], 64
    nodes, width = free_vec_ref.shape
    rows, emb = emb_ref.shape
    length = rows // (queries + labels)
    q_rows = queries * length
    channels = w3_ref.shape[1]
    wide = all_q.shape[-1]

    loads = [
        pltpu.make_async_copy(src, dst, load_sem.at[i])
        for i, (src, dst) in enumerate(((w3_hbm, w3_ref), (w5_hbm, w5_ref), (proj_hbm, proj_ref)))
    ]
    for load in loads:
        load.start()

    def nt(a, b):
        return lax.dot_general(a, b, (((1,), (1,)), ((), ())), preferred_element_type=f32)

    def tn(a, b):
        return lax.dot_general(a, b, (((0,), (0,)), ((), ())), preferred_element_type=f32)

    def unfold(base, titles):
        size = titles * length
        for k in range(5):
            move = (k - 2) * titles
            low, high = max(0, -move), size - max(0, move)
            columns = pl.ds(k * emb, emb)
            if low:
                taps[pl.ds(base, low), columns] = jnp.zeros((low, emb), bf16)
            taps[pl.ds(base + low, high - low), columns] = emb_ref[pl.ds(base + low + move, high - low), :]
            if high < size:
                taps[pl.ds(base + high, size - high), columns] = jnp.zeros((size - high, emb), bf16)

    def convolve(base, titles, first):
        block = 512
        for col in range(0, 2 * channels, 256):
            if col < channels:
                pre = jnp.dot(
                    taps[pl.ds(base, block), emb : 4 * emb], w3_ref[:, col : col + 256],
                    preferred_element_type=f32,
                )
            else:
                pre = jnp.dot(
                    taps[pl.ds(base, block), :], w5_ref[:, col - channels : col - channels + 256],
                    preferred_element_type=f32,
                )
            bend = (ROOT * CUBIC) * (pre * pre)
            inner = bend + ROOT
            tanh = jnp.tanh(pre * inner)
            gate = 1.0 + tanh
            value = pre * gate
            slope[pl.ds(base, block), col : col + 256] = gate + value * (1.0 - tanh) * (inner + (bend + bend))
            part = jnp.sum(value.reshape(block // titles, titles, 256), axis=0)
            where = pl.ds(0 if titles == queries else queries, titles)
            if first:
                total[where, col : col + 256] = part
            else:
                total[where, col : col + 256] += part

    def encoded_of(where):
        pooled = (total[where, :] * (0.5 / length)).astype(bf16)
        pooled_ref[where, :] = pooled
        return jnp.dot(pooled, proj_ref[...], preferred_element_type=f32)

    def region(ref, part, phase, place, columns, spread=slice(None)):
        free = ORDERS[part][:phase]
        z, y, x = [slice(None) if a in free else place[a] for a in "zyx"]
        return ref.at[z, place["c"], y, x, spread, pl.ds(*columns)]

    started = []

    def push(ref, send, recv, slot, peer):
        copy = pltpu.make_async_remote_copy(
            src_ref=ref,
            dst_ref=ref,
            send_sem=send.at[slot],
            recv_sem=recv.at[slot],
            device_id=device_of(peer),
            device_id_type=MESH,
        )
        copy.start()
        started.append(copy)
        return copy

    def direct(ref, columns, send, recv, part, phase):
        here = region(ref, part, phase, at, columns[part])
        axis = ORDERS[part][phase]
        return [
            push(here, send, recv, (part, phase * 3 + d - 1), along(at, axis, d)) for d in STEPS
        ]

    def hand_over(ref, columns, group, part, d):
        there = region(ref, part, 2, along(at, ORDERS[part][2], d), columns[part])
        return push(there, over_send, over_recv, (group, part * 4 + d), partner)

    def wait_all(copies):
        for copy in copies:
            copy.wait_recv()

    barrier = pltpu.get_barrier_semaphore()
    peers = [along(at, axis, d) for axis in "xy" for d in (1, 2, 3)] + lab_peers
    for peer in peers:
        pl.semaphore_signal(barrier, inc=1, device_id=device_of(peer), device_id_type=MESH)
    unfold(0, queries)
    loads[0].wait()
    loads[1].wait()
    convolve(0, queries, True)
    convolve(512, queries, False)
    unfold(q_rows, labels)
    loads[2].wait()
    info = shortlist_codes(nodes_ref, listed_ref, owner_ref, positive_ref, nodes, labels)
    all_q[(*home, slice(None), pl.ds(0, width))] = encoded_of(pl.ds(0, queries)).astype(bf16)
    all_q[(*home, slice(None), pl.ds(width, wide - width))] = info.astype(bf16)
    pl.semaphore_wait(barrier, len(peers))
    q_stage = [direct(all_q, Q_PARTS, q_send, q_recv, part, 0) for part in range(3)]
    over = []

    convolve(q_rows, labels, True)
    for part in range(3):
        wait_all(q_stage[part])
        q_stage[part] = direct(all_q, Q_PARTS, q_send, q_recv, part, 1)
    convolve(q_rows + 512, labels, False)
    near = []
    for part in range(3):
        wait_all(q_stage[part])
        here = region(all_q, part, 2, at, Q_PARTS[part])
        axis = ORDERS[part][2]
        near.append(
            [push(here, q_send, q_recv, (part, 6 + k), along(at, axis, d)) for k, d in ((0, 1), (1, 3))]
        )
        over.append(hand_over(all_q, Q_PARTS, 0, part, 0))
    convolve(q_rows + 1024, labels, False)
    convolve(q_rows + 1536, labels, False)
    label_encoded = encoded_of(pl.ds(queries, labels))
    index = at["z"] * 32 + at["c"] * 16 + at["y"] * 4 + at["x"]
    pair = jnp.broadcast_to(nodes_ref[pl.ds(index // 2, 1), :].astype(f32), (nodes, 2 * labels))
    pair = jnp.where(lax.rem(index, 2) == 0, pair, pltpu.roll(pair, labels, 1))[:, :labels]
    member = lax.broadcasted_iota(jnp.int32, (nodes, labels), 0).astype(f32) == pair
    member = jnp.where(member, 1.0, 0.0)
    counts = jnp.sum(member, axis=1, keepdims=True)
    sums = jnp.dot(member, label_encoded, precision=lax.Precision.HIGHEST, preferred_element_type=f32)
    heads = (sums / counts + free_vec_ref[...].astype(f32)).astype(bf16)
    all_h[home] = heads
    h_stage = [direct(all_h, H_PARTS, h_send, h_recv, part, 0) for part in range(3)]
    far = []
    for part in range(3):
        axis = ORDERS[part][2]
        wait_all(near[part])
        for k, d in ((2, 1), (3, 3)):
            spread = pl.ds((k - 2) * (queries // 2), queries // 2)
            there = region(all_q, part, 2, along(at, axis, 4 - d), Q_PARTS[part], spread)
            far.append(push(there, q_send, q_recv, (part, 6 + k), along(at, axis, d)))
        over.append(hand_over(all_q, Q_PARTS, 0, part, 3))
        over.append(hand_over(all_q, Q_PARTS, 0, part, 1))
    for part in range(3):
        wait_all(h_stage[part])
        h_stage[part] = direct(all_h, H_PARTS, h_send, h_recv, part, 1)

    lane = lax.rem(lax.broadcasted_iota(jnp.int32, (queries, 128), 1), nodes).astype(f32)
    for k in range(8):
        tile = jnp.zeros((queries, 128), f32)
        for h in range(8):
            code = info[:, k * 8 + h : k * 8 + h + 1]
            tile += jnp.where(code == lane, 1.0, 0.0) + jnp.where(code == lane + nodes, 2.0, 0.0)
        tiles[k] = tile

    h_over = []
    for part in range(3):
        wait_all(h_stage[part])
        h_stage[part] = direct(all_h, H_PARTS, h_send, h_recv, part, 2)
        h_over.append(hand_over(all_h, H_PARTS, 1, part, 0))
    for part in range(3):
        wait_all(far[2 * part : 2 * part + 2])
        over.append(hand_over(all_q, Q_PARTS, 0, part, 2))
    wait_all(over)

    me = index.astype(f32)
    fold_row = lax.broadcasted_iota(jnp.int32, (8, 128), 0)
    fold_col = lax.broadcasted_iota(jnp.int32, (8, 128), 1)
    fold = jnp.where((lax.rem(fold_col, 8) == fold_row) & (fold_col < 64), 1.0, 0.0).astype(bf16)
    free_acc[...] = jnp.zeros_like(free_acc)
    grad_acc[...] = jnp.zeros_like(grad_acc)
    loss_acc[...] = jnp.zeros_like(loss_acc)
    node = lax.broadcasted_iota(jnp.int32, (nodes, 512), 0).astype(f32) + 1.0

    @pl.loop(0, 8, unroll=4)
    def _(i):
        chunk = all_q[i // 2, i % 2].reshape(512, wide)
        keys = chunk[:, :width]
        note = chunk[:, width:].astype(f32)
        owner = pltpu.roll(note, 64, 1)
        mine = jnp.where(owner == me, note + 1.0, 0.0).astype(bf16)
        listed = nt(fold, mine)
        scores = SCORE_SCALE * nt(all_h[home], keys)
        live = jnp.zeros((nodes, 512), f32)
        target = jnp.zeros((nodes, 512), f32)
        for h in range(8):
            entry = listed[h : h + 1]
            hit = jnp.where(entry == node + nodes, 1.0, 0.0)
            target += hit
            live += jnp.where(entry == node, 1.0, hit)
        weight = (SCORE_SCALE * (jax.nn.sigmoid(scores) - target) * live).astype(bf16)
        free_acc[...] += jnp.dot(weight, keys, preferred_element_type=f32)

    for k, d in enumerate(STEPS):
        for part in range(3):
            h_stage[part][k].wait_recv()
            h_over.append(hand_over(all_h, H_PARTS, 1, part, 4 - d))
    wait_all(h_over)

    own_rows = all_q[(*home, slice(None), pl.ds(0, width))]

    @pl.loop(0, 8, unroll=4)
    def _(i):
        keys = all_h[i // 2, i % 2].reshape(256, width)
        scores = SCORE_SCALE * nt(own_rows, keys)
        place = (lax.broadcasted_iota(jnp.int32, (queries, 256), 1) // nodes + i * (256 // nodes)).astype(f32)
        code = jnp.zeros((queries, 256), f32)
        for k in range(8):
            tile = tiles[k]
            pair = jnp.concatenate([tile, tile], axis=1)
            code += jnp.where(info[:, 64 + k * 8 : 65 + k * 8] == place, pair, 0.0)
        target = jnp.where(code > 1.5, 1.0, 0.0)
        live = jnp.where(code > 0.5, 1.0, 0.0)
        small = jnp.exp(-jnp.abs(scores))
        softplus = jnp.maximum(scores, 0.0) + jnp.log1p(small)
        loss_acc[...] += live * (softplus - target * scores)
        weight = (SCORE_SCALE * (jax.nn.sigmoid(scores) - target) * live).astype(bf16)
        grad_acc[...] += jnp.dot(weight, keys, preferred_element_type=f32)

    loss = jnp.sum(loss_acc[...], axis=1, keepdims=True)
    same = (queries, queries)
    eye = lax.broadcasted_iota(jnp.int32, same, 0) == lax.broadcasted_iota(jnp.int32, same, 1)
    loss_ref[...] = jnp.sum(jnp.where(eye, loss, 0.0), axis=0, keepdims=True)
    free = free_acc[...]
    free_ref[...] = free
    label_up = tn(member.astype(bf16), (free / counts).astype(bf16))
    upstream = jnp.concatenate([grad_acc[...].astype(bf16), label_up.astype(bf16)], axis=0)

    sent = []
    lane_of = lambda place: pl.ds(pl.multiple_of(128 * place, 128), 128)

    def ship(wave, part, phase, view, land):
        axis = ORDERS[part][phase]
        copies = []
        for d in STEPS:
            slot = phase * 3 + d - 1
            copy = pltpu.make_async_remote_copy(
                src_ref=view(lax.rem(at[axis] + d, 4)),
                dst_ref=land.at[d - 1],
                send_sem=send_sem.at[wave * 3 + part, slot],
                recv_sem=recv_sem.at[wave * 3 + part, slot],
                device_id=device_of(along(at, axis, d)),
                device_id_type=MESH,
            )
            copy.start()
            copies.append(copy)
        sent.extend(copies)
        return copies

    def add(target, mine, land, steps):
        for k in range(steps):
            target[k] = (mine(k) + land[0, k]) + (land[1, k] + land[2, k])

    def reduce_wave(wave, out_ref):
        own, other, done, parts = waves[wave]
        swaps = []
        for i in range(2):
            columns = pl.ds(256 * i, 256)
            swap = pltpu.make_async_remote_copy(
                src_ref=own.at[:, :, 1 - core, :, :, columns],
                dst_ref=other.at[:, :, :, :, columns],
                send_sem=core_send.at[wave, i],
                recv_sem=core_recv.at[wave, i],
                device_id=device_of(partner),
                device_id_type=MESH,
            )
            swap.start()
            swaps.append(swap)
            yield
        sent.extend(swaps)
        wait_all(swaps)
        for yy in range(4):
            for xx in range(4):
                own[yy, xx, core] += other[yy, xx]

        x, y, z = at["x"], at["y"], at["z"]
        us = [pl.ds(*units) for units in WAVE_UNITS[wave]]
        (r1x, bx, r2x, cx, r3x), (r1y, by, r2y, cy, r3y), (r1z, bz, r2z, cz, r3z) = parts
        waiting = [
            ship(wave, 0, 0, lambda p: own.at[:, p, core, us[0]], r1x),
            ship(wave, 1, 0, lambda p: own.at[p, :, core, us[1]], r1y),
            ship(wave, 2, 0, lambda p: own.at[:, :, core, us[2], :, lane_of(p)], r1z),
        ]
        yield
        wait_all(waiting[0])
        add(bx, lambda k: own[k, x, core, us[0]], r1x, 4)
        waiting[0] = ship(wave, 0, 1, lambda p: bx.at[p], r2x)
        wait_all(waiting[1])
        add(by, lambda k: own[y, k, core, us[1]], r1y, 4)
        waiting[1] = ship(wave, 1, 1, lambda p: by.at[:, :, :, lane_of(p)], r2y)
        wait_all(waiting[2])
        for xx in range(4):
            for k in range(4):
                first = own[k, xx, core, us[2], :, lane_of(z)]
                bz[k, xx] = (first + r1z[0, k, xx]) + (r1z[1, k, xx] + r1z[2, k, xx])

        waiting[2] = ship(wave, 2, 1, lambda p: bz.at[:, p], r2z)
        yield
        wait_all(waiting[0])
        cx[...] = (bx[y] + r2x[0]) + (r2x[1] + r2x[2])
        waiting[0] = ship(wave, 0, 2, lambda p: cx.at[:, :, lane_of(p)], r3x)
        wait_all(waiting[1])
        add(cy, lambda k: by[k, :, :, lane_of(z)], r2y, 4)
        waiting[1] = ship(wave, 1, 2, lambda p: cy.at[p], r3y)
        wait_all(waiting[2])
        add(cz, lambda k: bz[k, x], r2z, 4)
        waiting[2] = ship(wave, 2, 2, lambda p: cz.at[p], r3z)
        yield
        wait_all(waiting[0])
        done[us[0]] = (cx[:, :, lane_of(z)] + r3x[0]) + (r3x[1] + r3x[2])
        wait_all(waiting[1])
        done[us[1]] = (cy[x] + r3y[0]) + (r3y[1] + r3y[2])
        wait_all(waiting[2])
        done[us[2]] = (cz[y] + r3z[0]) + (r3z[1] + r3z[2])
        place = out_ref.at[core, :, :, lane_of(z)]
        final = []
        for i, peer in enumerate(lab_peers):
            copy = pltpu.make_async_remote_copy(
                src_ref=done,
                dst_ref=place,
                send_sem=out_send.at[wave, i],
                recv_sem=out_recv.at[wave, i],
                device_id=device_of(peer),
                device_id_type=MESH,
            )
            copy.start()
            final.append(copy)
        out_ref[core, :, :, lane_of(z)] = done[...]
        yield
        for copy in final:
            copy.wait()
        yield

    gp_ref, g5_ref, g3_ref = (waves[i][0] for i in range(3))
    gp_ref[...] = tn(pooled_ref[...], upstream).reshape(gp_ref.shape)
    move_p, move_5, move_3 = (reduce_wave(i, ref) for i, ref in enumerate((outp_ref, out5_ref, out3_ref)))
    next(move_p)
    next(move_p)
    grad_pooled = nt(upstream, proj_ref[...]) * (0.5 / length)

    def spread_back(low):
        for base, titles in ((0, queries), (q_rows, labels)):
            where = pl.ds(0 if titles == queries else queries, titles)
            mine = grad_pooled[:queries] if titles == queries else grad_pooled[queries:]
            mine = mine[:, low : low + channels]

            @pl.loop(0, length)
            def _(p):
                span = pl.ds(pl.multiple_of(base + p * titles, 32), titles)
                grad_pre[span, low : low + channels] = (
                    slope[span, low : low + channels] * mine
                ).astype(bf16)

    def weigh(ref, left, low):
        right = grad_pre[:, low : low + 256]
        col = low % channels
        ref[:, :, :, :, :, col : col + 256] = tn(left(), right).reshape(ref.shape[:-1] + (256,))

    spread_back(channels)
    next(move_p)
    weigh(g5_ref, lambda: taps[...], channels)
    next(move_5)
    weigh(g5_ref, lambda: taps[...], channels + 256)
    next(move_5)
    spread_back(0)
    next(move_5)
    weigh(g3_ref, lambda: taps[:, emb : 4 * emb], 0)
    next(move_3)
    weigh(g3_ref, lambda: taps[:, emb : 4 * emb], 256)
    next(move_3)
    next(move_p)
    next(move_3)
    for move in (move_p, move_5, move_3, move_p, move_5, move_3, move_5, move_3):
        next(move)
    for move in (move_p, move_5, move_3):
        next(move)
    for copy in started + sent:
        copy.wait_send()


def copy_out_kernel(*refs):
    for source, target in zip(refs[: len(refs) // 2], refs[len(refs) // 2 :]):
        target[...] = source[...]


def wave_scratch(units, width):
    f32 = jnp.float32
    count = sum(n for _, n in units)
    nx, ny, nz = (n for _, n in units)

    def pads(*shapes):
        return [pltpu.VMEM(shape, f32) for shape in shapes]

    return [
        pltpu.VMEM((4, 4, 2, count, 8, width), f32),
        pltpu.VMEM((4, 4, count, 8, width), f32),
        pltpu.VMEM((count, 8, 128), f32),
        [
            pads((3, 4, nx, 8, width), (4, nx, 8, width), (3, nx, 8, width), (nx, 8, width), (3, nx, 8, 128)),
            pads((3, 4, ny, 8, width), (4, ny, 8, width), (3, 4, ny, 8, 128), (4, ny, 8, 128), (3, ny, 8, 128)),
            pads(
                (3, 4, 4, nz, 8, 128), (4, 4, nz, 8, 128), (3, 4, nz, 8, 128), (4, nz, 8, 128), (3, nz, 8, 128)
            ),
        ],
    ]


def training_window(embedded, three, five, projection, label_node, listed, owner, positives, free_vectors):
    rows, emb = embedded.shape
    channels = three.shape[1]
    nodes, width = free_vectors.shape
    queries = listed.shape[1]
    titles = queries + 64
    f32, bf16 = jnp.float32, jnp.bfloat16
    vmem = pl.BlockSpec(memory_space=pltpu.VMEM)
    hbm = pl.BlockSpec(memory_space=pl.ANY)
    dma = pltpu.SemaphoreType.DMA
    shapes = (
        jax.ShapeDtypeStruct((1, queries), f32),
        jax.ShapeDtypeStruct((nodes, width), f32),
        jax.ShapeDtypeStruct((2, 3, 8, width), f32),
        jax.ShapeDtypeStruct((2, 5, 8, width), f32),
        jax.ShapeDtypeStruct((2, 4, 8, width), f32),
    )
    outs = pl.pallas_call(
        window_kernel,
        out_shape=shapes,
        in_specs=[vmem, hbm, hbm, hbm, vmem, vmem, vmem, vmem, vmem],
        out_specs=(vmem,) * 5,
        scratch_shapes=[
            pltpu.VMEM(three.shape, bf16),
            pltpu.VMEM(five.shape, bf16),
            pltpu.VMEM(projection.shape, bf16),
            pltpu.VMEM((rows, 5 * emb), bf16),
            pltpu.VMEM((rows, 2 * channels), f32),
            pltpu.VMEM((titles, 2 * channels), f32),
            pltpu.VMEM((titles, 2 * channels), bf16),
            pltpu.VMEM((4, 2, 4, 4, queries, width + 128), bf16),
            pltpu.VMEM((4, 2, 4, 4, nodes, width), bf16),
            pltpu.VMEM((nodes, width), f32),
            pltpu.VMEM((queries, width), f32),
            pltpu.VMEM((queries, 256), f32),
            pltpu.VMEM((8, queries, 128), f32),
            pltpu.VMEM((rows, 2 * channels), bf16),
            [wave_scratch(units, width) for units in WAVE_UNITS],
            dma((3,)),
            dma((3, 10)),
            dma((3, 10)),
            dma((3, 9)),
            dma((3, 9)),
            dma((2, 12)),
            dma((2, 12)),
            dma((3, 2)),
            dma((3, 2)),
            dma((9, 9)),
            dma((9, 9)),
            dma((3, 7)),
            dma((3, 7)),
        ],
        compiler_params=pltpu.CompilerParams(
            collective_id=1, has_side_effects=True, vmem_limit_bytes=60 << 20
        ),
        name="training_window",
    )(embedded, three, five, projection, label_node, listed, owner, positives, free_vectors)
    loss, grad_free, grad_three, grad_five, grad_projection = pl.pallas_call(
        copy_out_kernel,
        out_shape=shapes,
        in_specs=[vmem] * 5,
        out_specs=(vmem,) * 5,
        name="copy_out",
    )(*outs)
    return (
        loss.reshape(queries),
        grad_free,
        grad_three.reshape(48, width),
        grad_five.reshape(80, width),
        grad_projection.reshape(64, width),
    )


def per_device(
    query_tokens,
    label_tokens,
    label_node,
    shortlist_owner,
    shortlist_node,
    positives,
    table,
    three,
    five,
    projection,
    free_vectors,
):
    tokens = jnp.concatenate([query_tokens.T.reshape(-1), label_tokens.T.reshape(-1)])
    tokens = lax.optimization_barrier(tokens)
    embedded = table.at[tokens].get(mode="promise_in_bounds")
    return training_window(
        embedded,
        three,
        five,
        projection,
        label_node.reshape(-1, 128),
        shortlist_node.transpose(1, 2, 0).reshape(-1, query_tokens.shape[0]),
        shortlist_owner.T,
        positives.T,
        free_vectors,
    )


def solution(mesh):
    both = ("lab", "leaf")
    in_specs = (
        P(both, None),
        P(both, None),
        P(),
        P(both, None),
        P(both, None, None),
        P(both, None),
        P(),
        P(),
        P(),
        P(),
        P(both, None),
    )
    out_specs = (P(both), P(both, None), P("leaf", None), P("leaf", None), P("leaf", None))
    return jax.shard_map(
        per_device, mesh=mesh, in_specs=in_specs, out_specs=out_specs, check_vma=False
    )
```

```python
import jax
import jax.numpy as jnp
from jax import lax
from jax.experimental import pallas as pl
from jax.experimental.pallas import tpu as pltpu
from jax.sharding import PartitionSpec as P

MESH = pl.DeviceIdType.MESH
ORDERS = ("xyz", "yzx", "zxy")


SCORE_SCALE = 0.25


def where_am_i():
    lab, leaf = lax.axis_index("lab"), lax.axis_index("leaf")
    return {"z": lab // 2, "c": lab % 2, "y": leaf // 4, "x": leaf % 4}


def device_of(at):
    return (at["z"] * 2 + at["c"], at["y"] * 4 + at["x"])


def along(at, axis, step):
    size = 2 if axis == "c" else 4
    return {**at, axis: lax.rem(at[axis] + step, size)}


ROOT = 0.7978845608028654
CUBIC = 0.044715
Q_PARTS = ((0, 256), (256, 256), (512, 128))
H_PARTS = ((0, 128), (128, 128), (256, 256))
STEPS = (1, 3, 2)
WAVE_UNITS = (((0, 1), (1, 1), (2, 2)), ((0, 2), (2, 2), (4, 1)), ((0, 1), (1, 1), (2, 1)))


def shortlist_codes(nodes_ref, listed_ref, owner_ref, positive_ref, nodes, labels):
    bf16, f32 = jnp.bfloat16, jnp.float32
    count, queries = listed_ref.shape
    each = count // owner_ref.shape[0]
    listed = listed_ref[...]
    owners = jnp.concatenate(
        [jnp.broadcast_to(owner_ref[k : k + 1, :], (each, queries)) for k in range(count // each)], axis=0
    )
    table = nodes_ref[...].astype(f32).astype(bf16)
    lanes = table.shape[1]
    hit = jnp.zeros((count, queries), f32)
    for j in range(positive_ref.shape[0]):
        label = positive_ref[j : j + 1, :]
        row = lax.broadcasted_iota(jnp.int32, (table.shape[0], queries), 0) == label // lanes
        column = lax.broadcasted_iota(jnp.int32, (lanes, queries), 0) == label % lanes
        found = lax.dot_general(
            table, jnp.where(row, 1.0, 0.0).astype(bf16), (((0,), (0,)), ((), ())),
            preferred_element_type=f32,
        )
        node = jnp.sum(jnp.where(column, found, 0.0), axis=0, keepdims=True)
        same = (owners == label // labels) & (listed.astype(f32) == node)
        hit = jnp.where(same, 1.0, hit)
    codes = jnp.concatenate([listed.astype(f32) + nodes * hit, owners.astype(f32)], axis=0)
    square = (queries, queries)
    eye = lax.broadcasted_iota(jnp.int32, square, 0) == lax.broadcasted_iota(jnp.int32, square, 1)
    return lax.dot_general(
        jnp.where(eye, 1.0, 0.0).astype(bf16), codes.astype(bf16), (((1,), (1,)), ((), ())),
        preferred_element_type=f32,
    )


def window_kernel(
    emb_ref, w3_hbm, w5_hbm, proj_hbm, nodes_ref, listed_ref, owner_ref, positive_ref, free_vec_ref,
    loss_ref, free_ref, out3_ref, out5_ref, outp_ref,
    w3_ref, w5_ref, proj_ref, taps, slope, total, pooled_ref,
    all_q, all_h, free_acc, grad_acc, loss_acc, tiles,
    grad_pre, waves,
    load_sem, q_send, q_recv, h_send, h_recv, over_send, over_recv,
    core_send, core_recv, send_sem, recv_sem, out_send, out_recv,
):
    at = where_am_i()
    bf16, f32 = jnp.bfloat16, jnp.float32
    core = at["c"]
    partner = along(at, "c", 1)
    lab_steps = [(z, cc) for z in range(4) for cc in range(2)][1:]
    lab_peers = [along(along(at, "z", z), "c", cc) for z, cc in lab_steps]
    home = (at["z"], at["c"], at["y"], at["x"])
    queries, labels = listed_ref.shape[1], 64
    nodes, width = free_vec_ref.shape
    rows, emb = emb_ref.shape
    length = rows // (queries + labels)
    q_rows = queries * length
    channels = w3_ref.shape[1]
    wide = all_q.shape[-1]

    loads = [
        pltpu.make_async_copy(src, dst, load_sem.at[i])
        for i, (src, dst) in enumerate(((w3_hbm, w3_ref), (w5_hbm, w5_ref), (proj_hbm, proj_ref)))
    ]
    for load in loads:
        load.start()

    def nt(a, b):
        return lax.dot_general(a, b, (((1,), (1,)), ((), ())), preferred_element_type=f32)

    def tn(a, b):
        return lax.dot_general(a, b, (((0,), (0,)), ((), ())), preferred_element_type=f32)

    def unfold(base, titles):
        size = titles * length
        for k in range(5):
            move = (k - 2) * titles
            low, high = max(0, -move), size - max(0, move)
            columns = pl.ds(k * emb, emb)
            if low:
                taps[pl.ds(base, low), columns] = jnp.zeros((low, emb), bf16)
            taps[pl.ds(base + low, high - low), columns] = emb_ref[pl.ds(base + low + move, high - low), :]
            if high < size:
                taps[pl.ds(base + high, size - high), columns] = jnp.zeros((size - high, emb), bf16)

    def convolve(base, titles, first):
        block = 512
        for col in range(0, 2 * channels, 256):
            if col < channels:
                pre = jnp.dot(
                    taps[pl.ds(base, block), emb : 4 * emb], w3_ref[:, col : col + 256],
                    preferred_element_type=f32,
                )
            else:
                pre = jnp.dot(
                    taps[pl.ds(base, block), :], w5_ref[:, col - channels : col - channels + 256],
                    preferred_element_type=f32,
                )
            bend = (ROOT * CUBIC) * (pre * pre)
            inner = bend + ROOT
            tanh = jnp.tanh(pre * inner)
            gate = 1.0 + tanh
            value = pre * gate
            slope[pl.ds(base, block), col : col + 256] = gate + value * (1.0 - tanh) * (inner + (bend + bend))
            part = jnp.sum(value.reshape(block // titles, titles, 256), axis=0)
            where = pl.ds(0 if titles == queries else queries, titles)
            if first:
                total[where, col : col + 256] = part
            else:
                total[where, col : col + 256] += part

    def encoded_of(where):
        pooled = (total[where, :] * (0.5 / length)).astype(bf16)
        pooled_ref[where, :] = pooled
        return jnp.dot(pooled, proj_ref[...], preferred_element_type=f32)

    def region(ref, part, phase, place, columns, spread=slice(None)):
        free = ORDERS[part][:phase]
        z, y, x = [slice(None) if a in free else place[a] for a in "zyx"]
        return ref.at[z, place["c"], y, x, spread, pl.ds(*columns)]

    started = []

    def push(ref, send, recv, slot, peer):
        copy = pltpu.make_async_remote_copy(
            src_ref=ref,
            dst_ref=ref,
            send_sem=send.at[slot],
            recv_sem=recv.at[slot],
            device_id=device_of(peer),
            device_id_type=MESH,
        )
        copy.start()
        started.append(copy)
        return copy

    def direct(ref, columns, send, recv, part, phase):
        here = region(ref, part, phase, at, columns[part])
        axis = ORDERS[part][phase]
        return [
            push(here, send, recv, (part, phase * 3 + d - 1), along(at, axis, d)) for d in STEPS
        ]

    def hand_over(ref, columns, group, part, d):
        there = region(ref, part, 2, along(at, ORDERS[part][2], d), columns[part])
        return push(there, over_send, over_recv, (group, part * 4 + d), partner)

    def wait_all(copies):
        for copy in copies:
            copy.wait_recv()

    barrier = pltpu.get_barrier_semaphore()
    peers = [along(at, axis, d) for axis in "xy" for d in (1, 2, 3)] + lab_peers
    for peer in peers:
        pl.semaphore_signal(barrier, inc=1, device_id=device_of(peer), device_id_type=MESH)
    unfold(0, queries)
    loads[0].wait()
    loads[1].wait()
    convolve(0, queries, True)
    convolve(512, queries, False)
    unfold(q_rows, labels)
    loads[2].wait()
    info = shortlist_codes(nodes_ref, listed_ref, owner_ref, positive_ref, nodes, labels)
    all_q[(*home, slice(None), pl.ds(0, width))] = encoded_of(pl.ds(0, queries)).astype(bf16)
    all_q[(*home, slice(None), pl.ds(width, wide - width))] = info.astype(bf16)
    pl.semaphore_wait(barrier, len(peers))
    q_stage = [direct(all_q, Q_PARTS, q_send, q_recv, part, 0) for part in range(3)]
    over = []

    convolve(q_rows, labels, True)
    for part in range(3):
        wait_all(q_stage[part])
        q_stage[part] = direct(all_q, Q_PARTS, q_send, q_recv, part, 1)
    convolve(q_rows + 512, labels, False)
    near = []
    for part in range(3):
        wait_all(q_stage[part])
        here = region(all_q, part, 2, at, Q_PARTS[part])
        axis = ORDERS[part][2]
        near.append(
            [push(here, q_send, q_recv, (part, 6 + k), along(at, axis, d)) for k, d in ((0, 1), (1, 3))]
        )
        over.append(hand_over(all_q, Q_PARTS, 0, part, 0))
    convolve(q_rows + 1024, labels, False)
    convolve(q_rows + 1536, labels, False)
    label_encoded = encoded_of(pl.ds(queries, labels))
    index = at["z"] * 32 + at["c"] * 16 + at["y"] * 4 + at["x"]
    pair = jnp.broadcast_to(nodes_ref[pl.ds(index // 2, 1), :].astype(f32), (nodes, 2 * labels))
    pair = jnp.where(lax.rem(index, 2) == 0, pair, pltpu.roll(pair, labels, 1))[:, :labels]
    member = lax.broadcasted_iota(jnp.int32, (nodes, labels), 0).astype(f32) == pair
    member = jnp.where(member, 1.0, 0.0)
    counts = jnp.sum(member, axis=1, keepdims=True)
    sums = jnp.dot(member, label_encoded, precision=lax.Precision.HIGHEST, preferred_element_type=f32)
    heads = (sums / counts + free_vec_ref[...].astype(f32)).astype(bf16)
    all_h[home] = heads
    h_stage = [direct(all_h, H_PARTS, h_send, h_recv, part, 0) for part in range(3)]
    far = []
    for part in range(3):
        axis = ORDERS[part][2]
        wait_all(near[part])
        for k, d in ((2, 1), (3, 3)):
            spread = pl.ds((k - 2) * (queries // 2), queries // 2)
            there = region(all_q, part, 2, along(at, axis, 4 - d), Q_PARTS[part], spread)
            far.append(push(there, q_send, q_recv, (part, 6 + k), along(at, axis, d)))
        over.append(hand_over(all_q, Q_PARTS, 0, part, 3))
        over.append(hand_over(all_q, Q_PARTS, 0, part, 1))
    for part in range(3):
        wait_all(h_stage[part])
        h_stage[part] = direct(all_h, H_PARTS, h_send, h_recv, part, 1)

    lane = lax.rem(lax.broadcasted_iota(jnp.int32, (queries, 128), 1), nodes).astype(f32)
    for k in range(8):
        tile = jnp.zeros((queries, 128), f32)
        for h in range(8):
            code = info[:, k * 8 + h : k * 8 + h + 1]
            tile += jnp.where(code == lane, 1.0, 0.0) + jnp.where(code == lane + nodes, 2.0, 0.0)
        tiles[k] = tile

    h_over = []
    for part in range(3):
        wait_all(h_stage[part])
        h_stage[part] = direct(all_h, H_PARTS, h_send, h_recv, part, 2)
        h_over.append(hand_over(all_h, H_PARTS, 1, part, 0))
    for part in range(3):
        wait_all(far[2 * part : 2 * part + 2])
        over.append(hand_over(all_q, Q_PARTS, 0, part, 2))
    wait_all(over)

    me = index.astype(f32)
    fold_row = lax.broadcasted_iota(jnp.int32, (8, 128), 0)
    fold_col = lax.broadcasted_iota(jnp.int32, (8, 128), 1)
    fold = jnp.where((lax.rem(fold_col, 8) == fold_row) & (fold_col < 64), 1.0, 0.0).astype(bf16)
    free_acc[...] = jnp.zeros_like(free_acc)
    grad_acc[...] = jnp.zeros_like(grad_acc)
    loss_acc[...] = jnp.zeros_like(loss_acc)
    node = lax.broadcasted_iota(jnp.int32, (nodes, 512), 0).astype(f32) + 1.0

    @pl.loop(0, 8, unroll=8)
    def _(i):
        chunk = all_q[i // 2, i % 2].reshape(512, wide)
        keys = chunk[:, :width]
        note = chunk[:, width:].astype(f32)
        owner = pltpu.roll(note, 64, 1)
        mine = jnp.where(owner == me, note + 1.0, 0.0).astype(bf16)
        listed = nt(fold, mine)
        scores = SCORE_SCALE * nt(all_h[home], keys)
        live = jnp.zeros((nodes, 512), f32)
        target = jnp.zeros((nodes, 512), f32)
        for h in range(8):
            entry = listed[h : h + 1]
            hit = jnp.where(entry == node + nodes, 1.0, 0.0)
            target += hit
            live += jnp.where(entry == node, 1.0, hit)
        weight = (SCORE_SCALE * (jax.nn.sigmoid(scores) - target) * live).astype(bf16)
        free_acc[...] += jnp.dot(weight, keys, preferred_element_type=f32)

    for k, d in enumerate(STEPS):
        for part in range(3):
            h_stage[part][k].wait_recv()
            h_over.append(hand_over(all_h, H_PARTS, 1, part, 4 - d))
    wait_all(h_over)

    own_rows = all_q[(*home, slice(None), pl.ds(0, width))]

    @pl.loop(0, 8, unroll=8)
    def _(i):
        keys = all_h[i // 2, i % 2].reshape(256, width)
        scores = SCORE_SCALE * nt(own_rows, keys)
        place = (lax.broadcasted_iota(jnp.int32, (queries, 256), 1) // nodes + i * (256 // nodes)).astype(f32)
        code = jnp.zeros((queries, 256), f32)
        for k in range(8):
            tile = tiles[k]
            pair = jnp.concatenate([tile, tile], axis=1)
            code += jnp.where(info[:, 64 + k * 8 : 65 + k * 8] == place, pair, 0.0)
        target = jnp.where(code > 1.5, 1.0, 0.0)
        live = jnp.where(code > 0.5, 1.0, 0.0)
        small = jnp.exp(-jnp.abs(scores))
        softplus = jnp.maximum(scores, 0.0) + jnp.log1p(small)
        loss_acc[...] += live * (softplus - target * scores)
        weight = (SCORE_SCALE * (jax.nn.sigmoid(scores) - target) * live).astype(bf16)
        grad_acc[...] += jnp.dot(weight, keys, preferred_element_type=f32)

    loss = jnp.sum(loss_acc[...], axis=1, keepdims=True)
    same = (queries, queries)
    eye = lax.broadcasted_iota(jnp.int32, same, 0) == lax.broadcasted_iota(jnp.int32, same, 1)
    loss_ref[...] = jnp.sum(jnp.where(eye, loss, 0.0), axis=0, keepdims=True)
    free = free_acc[...]
    free_ref[...] = free
    label_up = tn(member.astype(bf16), (free / counts).astype(bf16))
    upstream = jnp.concatenate([grad_acc[...].astype(bf16), label_up.astype(bf16)], axis=0)

    sent = []
    lane_of = lambda place: pl.ds(pl.multiple_of(128 * place, 128), 128)

    def ship(wave, part, phase, view, land):
        axis = ORDERS[part][phase]
        copies = []
        for d in STEPS:
            slot = phase * 3 + d - 1
            copy = pltpu.make_async_remote_copy(
                src_ref=view(lax.rem(at[axis] + d, 4)),
                dst_ref=land.at[d - 1],
                send_sem=send_sem.at[wave * 3 + part, slot],
                recv_sem=recv_sem.at[wave * 3 + part, slot],
                device_id=device_of(along(at, axis, d)),
                device_id_type=MESH,
            )
            copy.start()
            copies.append(copy)
        sent.extend(copies)
        return copies

    def add(target, mine, land, steps):
        for k in range(steps):
            target[k] = (mine(k) + land[0, k]) + (land[1, k] + land[2, k])

    def reduce_wave(wave, out_ref):
        own, other, done, parts = waves[wave]
        swaps = []
        for i in range(2):
            columns = pl.ds(256 * i, 256)
            swap = pltpu.make_async_remote_copy(
                src_ref=own.at[:, :, 1 - core, :, :, columns],
                dst_ref=other.at[:, :, :, :, columns],
                send_sem=core_send.at[wave, i],
                recv_sem=core_recv.at[wave, i],
                device_id=device_of(partner),
                device_id_type=MESH,
            )
            swap.start()
            swaps.append(swap)
            yield
        sent.extend(swaps)
        wait_all(swaps)
        for yy in range(4):
            for xx in range(4):
                own[yy, xx, core] += other[yy, xx]

        x, y, z = at["x"], at["y"], at["z"]
        us = [pl.ds(*units) for units in WAVE_UNITS[wave]]
        (r1x, bx, r2x, cx, r3x), (r1y, by, r2y, cy, r3y), (r1z, bz, r2z, cz, r3z) = parts
        waiting = [
            ship(wave, 0, 0, lambda p: own.at[:, p, core, us[0]], r1x),
            ship(wave, 1, 0, lambda p: own.at[p, :, core, us[1]], r1y),
            ship(wave, 2, 0, lambda p: own.at[:, :, core, us[2], :, lane_of(p)], r1z),
        ]
        yield
        wait_all(waiting[0])
        add(bx, lambda k: own[k, x, core, us[0]], r1x, 4)
        waiting[0] = ship(wave, 0, 1, lambda p: bx.at[p], r2x)
        wait_all(waiting[1])
        add(by, lambda k: own[y, k, core, us[1]], r1y, 4)
        waiting[1] = ship(wave, 1, 1, lambda p: by.at[:, :, :, lane_of(p)], r2y)
        wait_all(waiting[2])
        for xx in range(4):
            for k in range(4):
                first = own[k, xx, core, us[2], :, lane_of(z)]
                bz[k, xx] = (first + r1z[0, k, xx]) + (r1z[1, k, xx] + r1z[2, k, xx])

        waiting[2] = ship(wave, 2, 1, lambda p: bz.at[:, p], r2z)
        yield
        wait_all(waiting[0])
        cx[...] = (bx[y] + r2x[0]) + (r2x[1] + r2x[2])
        waiting[0] = ship(wave, 0, 2, lambda p: cx.at[:, :, lane_of(p)], r3x)
        wait_all(waiting[1])
        add(cy, lambda k: by[k, :, :, lane_of(z)], r2y, 4)
        waiting[1] = ship(wave, 1, 2, lambda p: cy.at[p], r3y)
        wait_all(waiting[2])
        add(cz, lambda k: bz[k, x], r2z, 4)
        waiting[2] = ship(wave, 2, 2, lambda p: cz.at[p], r3z)
        yield
        wait_all(waiting[0])
        done[us[0]] = (cx[:, :, lane_of(z)] + r3x[0]) + (r3x[1] + r3x[2])
        wait_all(waiting[1])
        done[us[1]] = (cy[x] + r3y[0]) + (r3y[1] + r3y[2])
        wait_all(waiting[2])
        done[us[2]] = (cz[y] + r3z[0]) + (r3z[1] + r3z[2])
        place = out_ref.at[core, :, :, lane_of(z)]
        final = []
        for i, peer in enumerate(lab_peers):
            copy = pltpu.make_async_remote_copy(
                src_ref=done,
                dst_ref=place,
                send_sem=out_send.at[wave, i],
                recv_sem=out_recv.at[wave, i],
                device_id=device_of(peer),
                device_id_type=MESH,
            )
            copy.start()
            final.append(copy)
        out_ref[core, :, :, lane_of(z)] = done[...]
        yield
        for copy in final:
            copy.wait()
        yield

    gp_ref, g5_ref, g3_ref = (waves[i][0] for i in range(3))
    gp_ref[...] = tn(pooled_ref[...], upstream).reshape(gp_ref.shape)
    move_p, move_5, move_3 = (reduce_wave(i, ref) for i, ref in enumerate((outp_ref, out5_ref, out3_ref)))
    next(move_p)
    next(move_p)
    grad_pooled = nt(upstream, proj_ref[...]) * (0.5 / length)

    def spread_back(low):
        for base, titles in ((0, queries), (q_rows, labels)):
            where = pl.ds(0 if titles == queries else queries, titles)
            mine = grad_pooled[:queries] if titles == queries else grad_pooled[queries:]
            mine = mine[:, low : low + channels]

            @pl.loop(0, length, unroll=4)
            def _(p):
                span = pl.ds(pl.multiple_of(base + p * titles, 32), titles)
                grad_pre[span, low : low + channels] = (
                    slope[span, low : low + channels] * mine
                ).astype(bf16)

    def weigh(ref, left, low):
        right = grad_pre[:, low : low + 256]
        col = low % channels
        ref[:, :, :, :, :, col : col + 256] = tn(left(), right).reshape(ref.shape[:-1] + (256,))

    spread_back(channels)
    next(move_p)
    weigh(g5_ref, lambda: taps[...], channels)
    next(move_5)
    weigh(g5_ref, lambda: taps[...], channels + 256)
    next(move_5)
    spread_back(0)
    next(move_5)
    weigh(g3_ref, lambda: taps[:, emb : 4 * emb], 0)
    next(move_3)
    weigh(g3_ref, lambda: taps[:, emb : 4 * emb], 256)
    next(move_3)
    next(move_p)
    next(move_3)
    for move in (move_p, move_5, move_3, move_p, move_5, move_3, move_5, move_3):
        next(move)
    for move in (move_p, move_5, move_3):
        next(move)
    for copy in started + sent:
        copy.wait_send()


def copy_out_kernel(*refs):
    for source, target in zip(refs[: len(refs) // 2], refs[len(refs) // 2 :]):
        target[...] = source[...]


def wave_scratch(units, width):
    f32 = jnp.float32
    count = sum(n for _, n in units)
    nx, ny, nz = (n for _, n in units)

    def pads(*shapes):
        return [pltpu.VMEM(shape, f32) for shape in shapes]

    return [
        pltpu.VMEM((4, 4, 2, count, 8, width), f32),
        pltpu.VMEM((4, 4, count, 8, width), f32),
        pltpu.VMEM((count, 8, 128), f32),
        [
            pads((3, 4, nx, 8, width), (4, nx, 8, width), (3, nx, 8, width), (nx, 8, width), (3, nx, 8, 128)),
            pads((3, 4, ny, 8, width), (4, ny, 8, width), (3, 4, ny, 8, 128), (4, ny, 8, 128), (3, ny, 8, 128)),
            pads(
                (3, 4, 4, nz, 8, 128), (4, 4, nz, 8, 128), (3, 4, nz, 8, 128), (4, nz, 8, 128), (3, nz, 8, 128)
            ),
        ],
    ]


def training_window(embedded, three, five, projection, label_node, listed, owner, positives, free_vectors):
    rows, emb = embedded.shape
    channels = three.shape[1]
    nodes, width = free_vectors.shape
    queries = listed.shape[1]
    titles = queries + 64
    f32, bf16 = jnp.float32, jnp.bfloat16
    vmem = pl.BlockSpec(memory_space=pltpu.VMEM)
    hbm = pl.BlockSpec(memory_space=pl.ANY)
    dma = pltpu.SemaphoreType.DMA
    shapes = (
        jax.ShapeDtypeStruct((1, queries), f32),
        jax.ShapeDtypeStruct((nodes, width), f32),
        jax.ShapeDtypeStruct((2, 3, 8, width), f32),
        jax.ShapeDtypeStruct((2, 5, 8, width), f32),
        jax.ShapeDtypeStruct((2, 4, 8, width), f32),
    )
    outs = pl.pallas_call(
        window_kernel,
        out_shape=shapes,
        in_specs=[vmem, hbm, hbm, hbm, vmem, vmem, vmem, vmem, vmem],
        out_specs=(vmem,) * 5,
        scratch_shapes=[
            pltpu.VMEM(three.shape, bf16),
            pltpu.VMEM(five.shape, bf16),
            pltpu.VMEM(projection.shape, bf16),
            pltpu.VMEM((rows, 5 * emb), bf16),
            pltpu.VMEM((rows, 2 * channels), f32),
            pltpu.VMEM((titles, 2 * channels), f32),
            pltpu.VMEM((titles, 2 * channels), bf16),
            pltpu.VMEM((4, 2, 4, 4, queries, width + 128), bf16),
            pltpu.VMEM((4, 2, 4, 4, nodes, width), bf16),
            pltpu.VMEM((nodes, width), f32),
            pltpu.VMEM((queries, width), f32),
            pltpu.VMEM((queries, 256), f32),
            pltpu.VMEM((8, queries, 128), f32),
            pltpu.VMEM((rows, 2 * channels), bf16),
            [wave_scratch(units, width) for units in WAVE_UNITS],
            dma((3,)),
            dma((3, 10)),
            dma((3, 10)),
            dma((3, 9)),
            dma((3, 9)),
            dma((2, 12)),
            dma((2, 12)),
            dma((3, 2)),
            dma((3, 2)),
            dma((9, 9)),
            dma((9, 9)),
            dma((3, 7)),
            dma((3, 7)),
        ],
        compiler_params=pltpu.CompilerParams(
            collective_id=1, has_side_effects=True, vmem_limit_bytes=60 << 20
        ),
        name="training_window",
    )(embedded, three, five, projection, label_node, listed, owner, positives, free_vectors)
    loss, grad_free, grad_three, grad_five, grad_projection = pl.pallas_call(
        copy_out_kernel,
        out_shape=shapes,
        in_specs=[vmem] * 5,
        out_specs=(vmem,) * 5,
        name="copy_out",
    )(*outs)
    return (
        loss.reshape(queries),
        grad_free,
        grad_three.reshape(48, width),
        grad_five.reshape(80, width),
        grad_projection.reshape(64, width),
    )


def per_device(
    query_tokens,
    label_tokens,
    label_node,
    shortlist_owner,
    shortlist_node,
    positives,
    table,
    three,
    five,
    projection,
    free_vectors,
):
    tokens = jnp.concatenate([query_tokens.T.reshape(-1), label_tokens.T.reshape(-1)])
    tokens = lax.optimization_barrier(tokens)
    embedded = table.at[tokens].get(mode="promise_in_bounds")
    return training_window(
        embedded,
        three,
        five,
        projection,
        label_node.reshape(-1, 128),
        shortlist_node.transpose(1, 2, 0).reshape(-1, query_tokens.shape[0]),
        shortlist_owner.T,
        positives.T,
        free_vectors,
    )


def solution(mesh):
    both = ("lab", "leaf")
    in_specs = (
        P(both, None),
        P(both, None),
        P(),
        P(both, None),
        P(both, None, None),
        P(both, None),
        P(),
        P(),
        P(),
        P(),
        P(both, None),
    )
    out_specs = (P(both), P(both, None), P("leaf", None), P("leaf", None), P("leaf", None))
    return jax.shard_map(
        per_device, mesh=mesh, in_specs=in_specs, out_specs=out_specs, check_vma=False
    )
```
